256 devices in a mesh: ctx: 128 (over x_lo, y, z, core), head: 2 (over x_hi).
Axes of the slice: x: 4 (x_hi: 2, x_lo: 2; x = x_hi * 2 + x_lo), y: 4, z: 8, core: 2. Of those that a mesh axis runs over, the one named last changes fastest.
Arguments:
- queries: bfloat16 [65536, 8, 4, 128], P('ctx', None, 'head'), may hold values from -6 to 6
- key_heads: bfloat16 [65536, 8, 128], P('ctx'), may hold values from -6 to 6
- value_heads: bfloat16 [65536, 8, 128], P('ctx'), may hold values from -6 to 6
- out_grad: bfloat16 [65536, 8, 4, 128], P('ctx', None, 'head'), may hold values from -6 to 6
- doc_ids: int32 [65536], P('ctx'), may hold values from 0 to 255, never falling along the last dimension, each value on 1 to 2048 neighbouring positions
Outputs:
- query_grad: bfloat16 [65536, 8, 4, 128], P('ctx', None, 'head')
- key_grad: bfloat16 [65536, 8, 128], P('ctx', 'head')
- value_grad: bfloat16 [65536, 8, 128], P('ctx', 'head')
The draws below stay inside these ranges and needn't reach their ends.
Inputs may be any that keep to these rules, and one draw needn't show every extreme that they name: `doc_ids`: ids never fall along the sequence; a document has at most 2048 tokens.
All inputs are finite; a program needn't handle non-finite values.
Results may differ from the reference program's by a relative error of at most 0.012.
Values may be sent and summed in bfloat16 or wider, within the bound.
A program may use at most 64 MiB of HBM per device.

```python
import math
import jax
import jax.numpy as jnp
import numpy as np
from jax import lax

KV = 8
GROUP = 4
HD = 128
WINDOW = 256
TOK_DEV = 512
TOKENS = 65536
DOCS = 256
N_CTX = 128


def draw_queries(key, part):
    own_key = jax.random.fold_in(key, 1)
    result = jnp.clip(jax.random.normal(own_key, (TOKENS, KV, GROUP, HD), jnp.float32), -6.0, 6.0)
    return result.astype(jnp.bfloat16)


def draw_key_heads(key, part):
    own_key = jax.random.fold_in(key, 2)
    result = jnp.clip(jax.random.normal(own_key, (TOKENS, KV, HD), jnp.float32), -6.0, 6.0)
    return result.astype(jnp.bfloat16)


def block_levels(key, extent, shards, smallest, largest):
    factor_of = 1.0
    for position, blocks in shards:
        draws = jax.random.uniform(jax.random.fold_in(jax.random.fold_in(key, 6), position), (blocks,), jnp.float32, smallest / len(shards), largest / len(shards))
        factor_of = factor_of * jnp.repeat(jnp.exp(draws), extent[position] // blocks).reshape((-1,) + (1,) * (len(extent) - 1 - position))
    return factor_of


def profile(count, total, limit, lean):
    weights = [(1 << 20) // math.isqrt(rank ** lean) + 1 for rank in range(2, count + 1)]
    spare, holding = total - limit - (count - 1), [1] * (count - 1)
    while spare > 0:
        free = [i for i in range(count - 1) if holding[i] < limit]
        whole, remaining = sum([weights[i] for i in free]), spare
        for i in free:
            extra = min(limit - holding[i], max(1, remaining * weights[i] // whole), spare)
            holding[i] = holding[i] + extra
            spare = spare - extra
    return np.array([limit] + holding)


def ragged_sizes(key, count, total, reach, lean):
    if count == 2:
        one = jax.random.randint(key, (), max(1, total - reach), min(reach, total - 1) + 1)
        return jnp.stack([one, total - one])
    lengths = jnp.asarray(profile(count, total, reach, lean), jnp.int32)
    twos = (count - 1) // 2
    giver, sink = lengths[1:1 + 2 * twos:2], lengths[2:2 + 2 * twos:2]
    margin = jnp.minimum(giver - 1, reach - sink)
    moved = jax.random.randint(jax.random.fold_in(key, 1), (twos,), 0, 1 << 20) % (margin + 1)
    lengths = lengths.at[1:1 + 2 * twos:2].set(giver - moved).at[2:2 + 2 * twos:2].set(sink + moved)
    return lengths[jax.random.permutation(jax.random.fold_in(key, 2), count)]


def bell_draw(stream_key, shape, scale, limit, pieces=(), kind=jnp.bfloat16):
    array = scale * jax.random.normal(stream_key, shape, jnp.float32)
    if pieces:
        array = array * block_levels(stream_key, shape, pieces, -0.22, 0.18)
    return jnp.clip(array, -limit, limit).astype(kind)


def setup_inputs(seed: int = 0) -> dict:
    key_list = jax.random.split(jax.random.key(seed), 6)
    queries = draw_queries(jax.random.fold_in(key_list[5], 71), 0)
    key_heads = draw_key_heads(jax.random.fold_in(key_list[5], 71), 0)
    value_heads = bell_draw(key_list[2], (TOKENS, KV, HD), 1.0, 6.0, ((0, 128),))
    out_grad = bell_draw(key_list[3], (TOKENS, KV, GROUP, HD), 1.0, 6.0, ((0, 128), (2, 2)))
    doc_ids = jnp.searchsorted(jnp.cumsum(ragged_sizes(key_list[4], DOCS, TOKENS, 4 * TOK_DEV, 2)), jnp.arange(TOKENS), side="right").astype(jnp.int32)
    return dict(queries=queries, key_heads=key_heads, value_heads=value_heads, out_grad=out_grad, doc_ids=doc_ids)


def window_grads(query_blk, key_win, value_win, grad_blk, pos_query, pos_key, doc_query, doc_key):
    scaling = 1.0 / (HD ** 0.5)
    lag_rows = pos_query[:, None] - pos_key[None, :]
    visible = (lag_rows >= 0) & (lag_rows < WINDOW) & (doc_query[:, None] == doc_key[None, :]) & (pos_key[None, :] >= 0)
    query_f = query_blk.astype(jnp.float32)
    key_f = key_win.astype(jnp.float32)
    value_f = value_win.astype(jnp.float32)
    grad_f = grad_blk.astype(jnp.float32)
    scores = jnp.einsum("lngd,mnd->nglm", query_f, key_f) * scaling
    scores = jnp.where(visible[None, None], scores, -jnp.inf)
    top_score = jnp.max(scores, axis=-1, keepdims=True)
    weights = jnp.exp(scores - top_score)
    attn_prob = weights / jnp.sum(weights, axis=-1, keepdims=True)
    prob_low = lax.optimization_barrier(attn_prob.astype(jnp.bfloat16)).astype(jnp.float32)
    attended = jnp.einsum("nglm,mnd->lngd", prob_low, value_f)
    row_delta = jnp.sum(grad_f * attended, axis=-1)
    grad_prob = jnp.einsum("lngd,mnd->nglm", grad_f, value_f)
    grad_scores = attn_prob * (grad_prob - jnp.transpose(row_delta, (1, 2, 0))[..., None])
    grad_low = lax.optimization_barrier(grad_scores.astype(jnp.bfloat16)).astype(jnp.float32)
    query_part = (jnp.einsum("nglm,mnd->lngd", grad_low, key_f) * scaling).astype(jnp.bfloat16)
    key_part = jnp.einsum("nglm,lngd->mnd", grad_low, query_f) * scaling
    value_part = jnp.einsum("nglm,lngd->mnd", prob_low, grad_f)
    return query_part, key_part, value_part


def reference(queries, key_heads, value_heads, out_grad, doc_ids):
    window_rows = TOK_DEV + WINDOW
    pad_keys = jnp.concatenate([jnp.zeros((WINDOW, KV, HD), key_heads.dtype), key_heads], 0)
    pad_values = jnp.concatenate([jnp.zeros((WINDOW, KV, HD), value_heads.dtype), value_heads], 0)
    doc_all = doc_ids.astype(jnp.int32)
    pad_docs = jnp.concatenate([jnp.full((WINDOW,), -1, jnp.int32), doc_all], 0)
    offsets = jnp.arange(window_rows, dtype=jnp.int32)
    query_rows = jnp.arange(TOK_DEV, dtype=jnp.int32)

    def scan_step(loop_state, block_idx):
        key_acc, value_acc = loop_state
        anchor = (block_idx * TOK_DEV).astype(jnp.int32)
        query_blk = lax.dynamic_slice_in_dim(queries, anchor, TOK_DEV, 0)
        grad_blk = lax.dynamic_slice_in_dim(out_grad, anchor, TOK_DEV, 0)
        key_win = lax.dynamic_slice_in_dim(pad_keys, anchor, window_rows, 0)
        value_win = lax.dynamic_slice_in_dim(pad_values, anchor, window_rows, 0)
        doc_query = lax.dynamic_slice_in_dim(doc_all, anchor, TOK_DEV, 0)
        doc_key = lax.dynamic_slice_in_dim(pad_docs, anchor, window_rows, 0)
        pos_query = anchor + query_rows
        pos_key = anchor - WINDOW + offsets
        query_part, key_part, value_part = window_grads(query_blk, key_win, value_win, grad_blk, pos_query, pos_key, doc_query, doc_key)
        key_acc = lax.dynamic_update_slice_in_dim(key_acc, lax.dynamic_slice_in_dim(key_acc, anchor, window_rows, 0) + key_part, anchor, 0)
        value_acc = lax.dynamic_update_slice_in_dim(value_acc, lax.dynamic_slice_in_dim(value_acc, anchor, window_rows, 0) + value_part, anchor, 0)
        return (key_acc, value_acc), query_part

    initial = (jnp.zeros((TOKENS + WINDOW, KV, HD), jnp.float32), jnp.zeros((TOKENS + WINDOW, KV, HD), jnp.float32))
    (key_acc, value_acc), query_parts = lax.scan(scan_step, initial, jnp.arange(N_CTX, dtype=jnp.int32))
    query_grad = query_parts.reshape(TOKENS, KV, GROUP, HD)
    return query_grad, key_acc[WINDOW:].astype(jnp.bfloat16), value_acc[WINDOW:].astype(jnp.bfloat16)
```

```python
import functools

import jax
import jax.numpy as jnp
from jax import lax
from jax.experimental import pallas as pl
from jax.experimental.pallas import tpu as pltpu
from jax.sharding import PartitionSpec as P

MESH = pl.DeviceIdType.MESH
WINDOW = 256
TOK = 512
KV = 8
HD = 128
HALF = 4
NCTX = 128
SCALE = HD**-0.5
EXP_SCALE = SCALE * 1.4426950408889634
HIDDEN = -1e30
NT = (((1,), (1,)), ((), ()))
NN = (((1,), (0,)), ((), ()))
TN = (((0,), (0,)), ((), ()))
bf16 = jnp.bfloat16
f32 = jnp.float32


def dot(a, b, dims):
    return lax.dot_general(a, b, dims, preferred_element_type=f32)


def attention_tile(q, g, k, v, mask, onehot):
    s = dot(jnp.concatenate([k, mask], 1), jnp.concatenate([q, onehot], 1), NT)
    dp = dot(v, g, NT)
    top = jnp.max(s, 0, keepdims=True)
    e = jnp.exp2((s - top) * EXP_SCALE)
    total = jnp.sum(e, 0, keepdims=True)
    moment = jnp.sum(e * dp, 0, keepdims=True)
    inv = 1.0 / total
    p = e * inv
    ds = (p * (dp - moment * inv)).astype(bf16)
    p = p.astype(bf16)
    dv = dot(p, g, NN)
    dk = dot(ds, q, NN)
    dq_t = dot(k, ds, TN)
    return (dq_t * SCALE).T.astype(bf16), dk, dv


def kernel(
    q_hbm, k_hbm, v_hbm, g_hbm, doc_ref,
    dq_hbm, dk_hbm, dv_hbm,
    q_raw, g_raw, k_raw, v_raw, kt, vt, mask, onehot, doc_halo, doc_col,
    dq_s, ak, av, edge_s, edge_r, xs, xr, out_k, out_v,
    in_sem, kv_sem, f_send, f_recv, d_send, d_recv, e_send, e_recv, x_send, x_recv, dq_sem, out_sem,
):
    c = lax.axis_index("ctx")
    h = lax.axis_index("head")
    par = lax.rem(c, 2)
    first, last = c == 0, c == NCTX - 1
    has_prev, has_next = c > 0, c < NCTX - 1
    partner, nxt, prv = (c, 1 - h), (c + 1, h), (c - 1, h)

    def remote(src, dst, send, recv, dev):
        return pltpu.make_async_remote_copy(
            src_ref=src, dst_ref=dst, send_sem=send, recv_sem=recv, device_id=dev, device_id_type=MESH
        )

    def head_of(grp, i):
        return HALF * jnp.where(grp == 0, 1 - h, h) + i

    barrier = pltpu.get_barrier_semaphore()
    pl.semaphore_signal(barrier, inc=1, device_id=partner, device_id_type=MESH)

    @pl.when(has_prev)
    def _():
        pl.semaphore_signal(barrier, inc=1, device_id=prv, device_id_type=MESH)

    @pl.when(par == 0)
    def _():
        pl.semaphore_signal(barrier, inc=1, device_id=nxt, device_id_type=MESH)

    def kv_copy(j, r):
        src, dst = ((k_hbm, k_raw), (v_hbm, v_raw))[j]
        rows = pl.ds(r * WINDOW, WINDOW)
        return pltpu.make_async_copy(src.at[rows], dst.at[rows], kv_sem.at[j, r])

    def q_copy(n):
        return pltpu.make_async_copy(q_hbm.at[:, n], q_raw.at[n], in_sem.at[0, n])

    def g_copy(n):
        return pltpu.make_async_copy(g_hbm.at[:, n], g_raw.at[n], in_sem.at[1, n])

    for r in (1, 0):
        for j in (0, 1):
            kv_copy(j, r).start()

    def start_loads(i, _):
        n = head_of(i // HALF, lax.rem(i, HALF))
        q_copy(n).start()
        g_copy(n).start()
        return 0

    lax.fori_loop(0, KV, start_loads, 0)

    def clear(n, _):
        ak[n] = jnp.zeros((TOK + WINDOW, HD), f32)
        av[n] = jnp.zeros((TOK + WINDOW, HD), f32)
        return 0

    lax.fori_loop(0, KV, clear, 0)

    row = lax.broadcasted_iota(jnp.int32, (256, 128), 0)
    col = lax.broadcasted_iota(jnp.int32, (256, 128), 1)
    onehot[...] = jnp.where(row // 2 == col, 1.0, 0.0).astype(bf16)

    @pl.when(first)
    def _():
        kt[:, :WINDOW] = jnp.zeros((KV, WINDOW, HD), bf16)
        vt[:, :WINDOW] = jnp.zeros((KV, WINDOW, HD), bf16)
        doc_halo[...] = jnp.full((4, 128), -1, jnp.int32)

    @pl.when(last)
    def _():
        edge_r[...] = jnp.zeros(edge_r.shape, bf16)

    def swap(src, dst, r):
        def body(b, _):
            t = pl.multiple_of(r * WINDOW + b * 32, 32)
            dst[:, pl.ds(pl.multiple_of(t + WINDOW, 32), 32)] = jnp.swapaxes(src[pl.ds(t, 32)], 0, 1)
            return 0

        lax.fori_loop(0, WINDOW // 32, body, 0)

    for j, src, dst in ((0, k_raw, kt), (1, v_raw, vt)):
        kv_copy(j, 1).wait()
        swap(src, dst, 1)

    def doc_copy():
        return remote(doc_ref, doc_halo, d_send, d_recv, nxt)

    def halo_copy(n, j):
        ref = (kt, vt)[j]
        return remote(
            ref.at[n, pl.ds(TOK, WINDOW)], ref.at[n, pl.ds(0, WINDOW)], f_send.at[j, n], f_recv.at[j, n], nxt
        )

    @pl.when(par == 0)
    def _():
        pl.semaphore_wait(barrier, 2)

    @pl.when((par == 1) & has_next)
    def _():
        pl.semaphore_wait(barrier, 3)

    @pl.when(last)
    def _():
        pl.semaphore_wait(barrier, 2)

    @pl.when(has_next)
    def _():
        doc_copy().start()

        def send_halo(i, _):
            n = head_of(i // HALF, lax.rem(i, HALF))
            halo_copy(n, 0).start()
            halo_copy(n, 1).start()
            return 0

        lax.fori_loop(0, KV, send_halo, 0)

    for j, src, dst in ((0, k_raw, kt), (1, v_raw, vt)):
        kv_copy(j, 0).wait()
        swap(src, dst, 0)

    key_row = lax.broadcasted_iota(jnp.int32, (128, 128), 0)
    tok_col = lax.broadcasted_iota(jnp.int32, (128, 128), 1)

    def doc_columns(block, ref, r):
        wide = jnp.broadcast_to(ref[r : r + 1, :], (128, 128)).astype(f32)
        doc_col[block] = wide.T

    def build_mask(t):
        docs = jnp.broadcast_to(doc_ref[t : t + 1, :], (128, 128)).astype(f32)
        for b, inside in enumerate((key_row > tok_col, None, key_row <= tok_col)):
            same = doc_col[t + b] == docs
            seen = same if inside is None else same & inside
            mask[t, b * 128 : (b + 1) * 128] = jnp.where(seen, 0.0, HIDDEN).astype(bf16)

    for b in range(4):
        doc_columns(2 + b, doc_ref, b)
    build_mask(2)
    build_mask(3)

    def edge_copy(n, j):
        return remote(edge_s.at[n, j], edge_r.at[n, j], e_send.at[j, n], e_recv.at[j, n], prv)

    def x_copy(i, r, j):
        return remote(xs.at[i, r, j], xr.at[i, r, j], x_send.at[i, r, j], x_recv.at[i, r, j], partner)

    def dq_copy(n):
        return pltpu.make_async_copy(dq_s.at[n], dq_hbm.at[:, n], dq_sem.at[n])

    def send_tail_sums(i):
        n = head_of(0, i)

        @pl.when(has_next)
        def _():
            edge_copy(n, 0).wait_recv()
            edge_copy(n, 1).wait_recv()

        xs[i, 1, 0] = (ak[n, TOK:] * SCALE + edge_r[n, 0].astype(f32)).astype(bf16)
        xs[i, 1, 1] = (av[n, TOK:] + edge_r[n, 1].astype(f32)).astype(bf16)
        x_copy(i, 1, 0).start()
        x_copy(i, 1, 1).start()

    def step(s, _):
        i = lax.rem(s, HALF)
        late = lax.rem(s // HALF, 2)
        grp = s // (2 * HALF)
        n = head_of(grp, i)
        crossing = late + par == 1
        t0 = 2 * jnp.where(late == 1, par, 1 - par)

        @pl.when(late == 0)
        def _():
            q_copy(n).wait()
            g_copy(n).wait()

        @pl.when(crossing & (i == 0) & (grp == 0))
        def _():
            @pl.when(has_prev)
            def _():
                doc_copy().wait_recv()

            doc_columns(0, doc_halo, 2)
            doc_columns(1, doc_halo, 3)
            build_mask(0)
            build_mask(1)

        @pl.when(crossing & has_prev)
        def _():
            halo_copy(n, 0).wait_recv()
            halo_copy(n, 1).wait_recv()

        res = []
        for j in range(2):
            t = t0 + j
            rows = pl.ds(pl.multiple_of(t * 256, 256), 256)
            keys = pl.ds(pl.multiple_of(t * 128, 128), 384)
            q = q_raw.at[n].reshape(1024, 128)[rows, :]
            g = g_raw.at[n].reshape(1024, 128)[rows, :]
            dq, dk, dv = attention_tile(q, g, kt[n, keys], vt[n, keys], mask[t], onehot[...])
            dq_s.at[n].reshape(1024, 128)[rows, :] = dq
            res.append((dk, dv))
        base = pl.ds(pl.multiple_of(t0 * 128, 128), TOK)
        for acc, x, y in ((ak, res[0][0], res[1][0]), (av, res[0][1], res[1][1])):
            acc[n, base] += jnp.concatenate([x[:128], x[128:] + y[:256], y[256:]], 0)

        @pl.when(crossing & has_prev)
        def _():
            edge_s[n, 0] = (ak[n, :WINDOW] * SCALE).astype(bf16)
            edge_s[n, 1] = av[n, :WINDOW].astype(bf16)
            edge_copy(n, 0).start()
            edge_copy(n, 1).start()

        @pl.when(late == 1)
        def _():
            dq_copy(n).start()

        @pl.when((late == 1) & (grp == 0))
        def _():
            xs[i, 0, 0] = (ak[n, WINDOW:TOK] * SCALE).astype(bf16)
            xs[i, 0, 1] = av[n, WINDOW:TOK].astype(bf16)
            x_copy(i, 0, 0).start()
            x_copy(i, 0, 1).start()

        @pl.when((par == 0) & (s >= 1) & (s <= HALF))
        def _():
            send_tail_sums(s - 1)

        @pl.when((par == 1) & (s >= 2 * HALF) & (s < 3 * HALF))
        def _():
            send_tail_sums(s - 2 * HALF)

        return 0

    lax.fori_loop(0, 4 * HALF, step, 0)

    def out_copy(j, r):
        src, dst = ((out_k, dk_hbm), (out_v, dv_hbm))[j]
        rows = pl.ds(r * WINDOW, WINDOW)
        return pltpu.make_async_copy(src.at[rows], dst.at[rows], out_sem.at[j, r])

    def finish(r):
        def wait_head(i, _):
            x_copy(i, r, 0).wait_recv()
            x_copy(i, r, 1).wait_recv()
            if r == 1:

                @pl.when(has_next)
                def _():
                    edge_copy(HALF * h + i, 0).wait_recv()
                    edge_copy(HALF * h + i, 1).wait_recv()

            return 0

        lax.fori_loop(0, HALF, wait_head, 0)
        own = pl.ds(HALF * h, HALF)

        def body(b, _):
            t = pl.multiple_of(b * 32, 32)
            part = pl.ds(t, 32)
            accs = pl.ds(pl.multiple_of((r + 1) * WINDOW + t, 32), 32)
            outs = pl.ds(pl.multiple_of(r * WINDOW + t, 32), 32)
            for j, acc, scale, out in ((0, ak, SCALE, out_k), (1, av, None, out_v)):
                val = acc[own, accs]
                if scale is not None:
                    val = val * scale
                val = val + xr[:, r, j, part].astype(f32)
                if r == 1:
                    val = val + edge_r[own, j, part].astype(f32)
                out[outs] = jnp.swapaxes(val.astype(bf16), 0, 1)
            return 0

        lax.fori_loop(0, WINDOW // 32, body, 0)
        out_copy(0, r).start()
        out_copy(1, r).start()

    @pl.when(par == 0)
    def _():
        finish(1)
        finish(0)

    @pl.when(par == 1)
    def _():
        finish(0)
        finish(1)

    @pl.when(has_next)
    def _():
        doc_copy().wait_send()

    def drain(n, _):
        @pl.when(has_next)
        def _():
            halo_copy(n, 0).wait_send()
            halo_copy(n, 1).wait_send()

        @pl.when(has_prev)
        def _():
            edge_copy(n, 0).wait_send()
            edge_copy(n, 1).wait_send()

        dq_copy(n).wait()
        return 0

    lax.fori_loop(0, KV, drain, 0)

    def drain_x(i, _):
        for r in range(2):
            for j in range(2):
                x_copy(i, r, j).wait_send()
        return 0

    lax.fori_loop(0, HALF, drain_x, 0)
    for r in range(2):
        for j in range(2):
            out_copy(j, r).wait()


def on_device(queries, key_heads, value_heads, out_grad, doc_ids):
    hbm = pl.BlockSpec(memory_space=pl.ANY)
    vmem = pl.BlockSpec(memory_space=pltpu.VMEM)
    dma = pltpu.SemaphoreType.DMA
    return pl.pallas_call(
        kernel,
        out_shape=(
            jax.ShapeDtypeStruct((TOK, KV, 2, HD), bf16),
            jax.ShapeDtypeStruct((TOK, HALF, HD), bf16),
            jax.ShapeDtypeStruct((TOK, HALF, HD), bf16),
        ),
        in_specs=[hbm, hbm, hbm, hbm, vmem],
        out_specs=(hbm, hbm, hbm),
        scratch_shapes=[
            pltpu.VMEM((KV, TOK, 2, HD), bf16),
            pltpu.VMEM((KV, TOK, 2, HD), bf16),
            pltpu.VMEM((TOK, KV, HD), bf16),
            pltpu.VMEM((TOK, KV, HD), bf16),
            pltpu.VMEM((KV, TOK + WINDOW, HD), bf16),
            pltpu.VMEM((KV, TOK + WINDOW, HD), bf16),
            pltpu.VMEM((4, 384, HD), bf16),
            pltpu.VMEM((256, HD), bf16),
            pltpu.VMEM((4, 128), jnp.int32),
            pltpu.VMEM((6, 128, 128), f32),
            pltpu.VMEM((KV, TOK, 2, HD), bf16),
            pltpu.VMEM((KV, TOK + WINDOW, HD), f32),
            pltpu.VMEM((KV, TOK + WINDOW, HD), f32),
            pltpu.VMEM((KV, 2, WINDOW, HD), bf16),
            pltpu.VMEM((KV, 2, WINDOW, HD), bf16),
            pltpu.VMEM((HALF, 2, 2, WINDOW, HD), bf16),
            pltpu.VMEM((HALF, 2, 2, WINDOW, HD), bf16),
            pltpu.VMEM((TOK, HALF, HD), bf16),
            pltpu.VMEM((TOK, HALF, HD), bf16),
            dma((2, KV)),
            dma((2, 2)),
            dma((2, KV)),
            dma((2, KV)),
            dma(()),
            dma(()),
            dma((2, KV)),
            dma((2, KV)),
            dma((HALF, 2, 2)),
            dma((HALF, 2, 2)),
            dma((KV,)),
            dma((2, 2)),
        ],
        compiler_params=pltpu.CompilerParams(
            collective_id=0, has_side_effects=True, vmem_limit_bytes=56 * 1024 * 1024
        ),
        cost_estimate=pl.CostEstimate(flops=8 * 10**9, bytes_accessed=9 * 2**20, transcendentals=3 * 10**6),
    )(queries, key_heads, value_heads, out_grad, doc_ids.reshape(4, 128))


def solution(mesh):
    return jax.shard_map(
        on_device,
        mesh=mesh,
        in_specs=(
            P("ctx", None, "head", None),
            P("ctx", None, None),
            P("ctx", None, None),
            P("ctx", None, "head", None),
            P("ctx"),
        ),
        out_specs=(P("ctx", None, "head", None), P("ctx", "head", None), P("ctx", "head", None)),
        check_vma=False,
    )
```

```python
import functools

import jax
import jax.numpy as jnp
from jax import lax
from jax.experimental import pallas as pl
from jax.experimental.pallas import tpu as pltpu
from jax.sharding import PartitionSpec as P

MESH = pl.DeviceIdType.MESH
WINDOW = 256
TOK = 512
KV = 8
HD = 128
HALF = 4
NCTX = 128
TURN = NCTX // 2
SCALE = HD**-0.5
EXP_SCALE = SCALE * 1.4426950408889634
HIDDEN = -1e30
PIECES = 4
NT = (((1,), (1,)), ((), ()))
NN = (((1,), (0,)), ((), ()))
TN = (((0,), (0,)), ((), ()))
bf16 = jnp.bfloat16
f32 = jnp.float32


def dot(a, b, dims):
    return lax.dot_general(a, b, dims, preferred_element_type=f32)


def attention_tile(q, g, k, v, mask, onehot):
    s = dot(jnp.concatenate([k, mask], 1), jnp.concatenate([q, onehot], 1), NT)
    dp = dot(v, g, NT)
    top = jnp.max(s, 0, keepdims=True)
    e = jnp.exp2((s - top) * EXP_SCALE)
    total = jnp.sum(e, 0, keepdims=True)
    moment = jnp.sum(e * dp, 0, keepdims=True)
    inv = 1.0 / total
    p = e * inv
    ds = (p * (dp - moment * inv)).astype(bf16)
    p = p.astype(bf16)
    dv = dot(p, g, NN)
    dk = dot(ds, q, NN)
    dq_t = dot(k, ds, TN)
    return (dq_t * SCALE).T.astype(bf16), dk, dv


def kernel(
    q_hbm, k_hbm, v_hbm, g_hbm, doc_ref,
    dq_hbm, dk_hbm, dv_hbm,
    q_raw, g_raw, k_raw, v_raw, kt, vt, mask, onehot, doc_halo, doc_col,
    dq_s, ak, av, edge_s, edge_r, xs, xr, out_k, out_v,
    in_sem, kv_sem, f_send, f_recv, d_send, d_recv, e_send, e_recv, x_send, x_recv, dq_sem, out_sem,
):
    c = lax.axis_index("ctx")
    h = lax.axis_index("head")
    par = lax.rem(c, 2)
    first, last = c == 0, c == NCTX - 1
    has_prev, has_next = c > 0, c < NCTX - 1
    before_turn, after_turn = c == TURN - 1, c == TURN
    partner, nxt, prv = (c, 1 - h), (c + 1, h), (c - 1, h)
    nxt_v = (c + 1, jnp.where(before_turn, 1 - h, h))

    def remote(src, dst, send, recv, dev):
        return pltpu.make_async_remote_copy(
            src_ref=src, dst_ref=dst, send_sem=send, recv_sem=recv, device_id=dev, device_id_type=MESH
        )

    def head_of(grp, i):
        return HALF * jnp.where(grp == 0, 1 - h, h) + i

    barrier = pltpu.get_barrier_semaphore()
    pl.semaphore_signal(barrier, inc=1, device_id=partner, device_id_type=MESH)

    @pl.when(has_prev)
    def _():
        pl.semaphore_signal(barrier, inc=1, device_id=prv, device_id_type=MESH)

    @pl.when(par == 0)
    def _():
        pl.semaphore_signal(barrier, inc=1, device_id=nxt, device_id_type=MESH)

    @pl.when(after_turn)
    def _():
        pl.semaphore_signal(barrier, inc=1, device_id=(c - 1, 1 - h), device_id_type=MESH)

    def kv_copy(j, r):
        src, dst = ((k_hbm, k_raw), (v_hbm, v_raw))[j]
        rows = pl.ds(r * WINDOW, WINDOW)
        return pltpu.make_async_copy(src.at[rows], dst.at[rows], kv_sem.at[j, r])

    def q_copy(n):
        return pltpu.make_async_copy(q_hbm.at[:, n], q_raw.at[n], in_sem.at[0, n])

    def g_copy(n):
        return pltpu.make_async_copy(g_hbm.at[:, n], g_raw.at[n], in_sem.at[1, n])

    for r in (1, 0):
        for j in (0, 1):
            kv_copy(j, r).start()

    def start_loads(i, _):
        n = head_of(i // HALF, lax.rem(i, HALF))
        q_copy(n).start()
        g_copy(n).start()
        return 0

    lax.fori_loop(0, KV, start_loads, 0)

    def clear(n, _):
        ak[n] = jnp.zeros((TOK + WINDOW, HD), f32)
        av[n] = jnp.zeros((TOK + WINDOW, HD), f32)
        return 0

    lax.fori_loop(0, KV, clear, 0)

    row = lax.broadcasted_iota(jnp.int32, (256, 128), 0)
    col = lax.broadcasted_iota(jnp.int32, (256, 128), 1)
    onehot[...] = jnp.where(row // 2 == col, 1.0, 0.0).astype(bf16)

    @pl.when(first)
    def _():
        kt[:, :WINDOW] = jnp.zeros((KV, WINDOW, HD), bf16)
        vt[:, :WINDOW] = jnp.zeros((KV, WINDOW, HD), bf16)
        doc_halo[...] = jnp.full((4, 128), -1, jnp.int32)

    @pl.when(last)
    def _():
        edge_r[...] = jnp.zeros(edge_r.shape, bf16)

    def swap(src, dst, r):
        def body(b, _):
            t = pl.multiple_of(r * WINDOW + b * 32, 32)
            dst[:, pl.ds(pl.multiple_of(t + WINDOW, 32), 32)] = jnp.swapaxes(src[pl.ds(t, 32)], 0, 1)
            return 0

        lax.fori_loop(0, WINDOW // 32, body, 0)

    for j, src, dst in ((0, k_raw, kt), (1, v_raw, vt)):
        kv_copy(j, 1).wait()
        swap(src, dst, 1)

    def doc_copy():
        return remote(doc_ref, doc_halo, d_send, d_recv, nxt)

    def halo_copy(n, j):
        ref = (kt, vt)[j]
        dev = (nxt, nxt_v)[j]
        return remote(
            ref.at[n, pl.ds(TOK, WINDOW)], ref.at[n, pl.ds(0, WINDOW)], f_send.at[j, n], f_recv.at[j, n], dev
        )

    @pl.when(par == 0)
    def _():
        pl.semaphore_wait(barrier, 2)

    @pl.when((par == 1) & has_next & jnp.logical_not(before_turn))
    def _():
        pl.semaphore_wait(barrier, 3)

    @pl.when(before_turn)
    def _():
        pl.semaphore_wait(barrier, 4)

    @pl.when(last)
    def _():
        pl.semaphore_wait(barrier, 2)

    @pl.when(has_next)
    def _():
        doc_copy().start()

        def send_halo(i, _):
            n = head_of(i // HALF, lax.rem(i, HALF))
            halo_copy(n, 0).start()
            halo_copy(n, 1).start()
            return 0

        lax.fori_loop(0, KV, send_halo, 0)

    for j, src, dst in ((0, k_raw, kt), (1, v_raw, vt)):
        kv_copy(j, 0).wait()
        swap(src, dst, 0)

    key_row = lax.broadcasted_iota(jnp.int32, (128, 128), 0)
    tok_col = lax.broadcasted_iota(jnp.int32, (128, 128), 1)

    def doc_columns(block, ref, r):
        wide = jnp.broadcast_to(ref[r : r + 1, :], (128, 128)).astype(f32)
        doc_col[block] = wide.T

    def build_mask(t):
        docs = jnp.broadcast_to(doc_ref[t : t + 1, :], (128, 128)).astype(f32)
        for b, inside in enumerate((key_row > tok_col, None, key_row <= tok_col)):
            same = doc_col[t + b] == docs
            seen = same if inside is None else same & inside
            mask[t, b * 128 : (b + 1) * 128] = jnp.where(seen, 0.0, HIDDEN).astype(bf16)

    for b in range(4):
        doc_columns(2 + b, doc_ref, b)
    build_mask(2)
    build_mask(3)

    def edge_copy(n, j):
        cross = after_turn & (n // HALF != h)
        slot = jnp.where(cross, lax.rem(n + HALF, KV), n)
        dev = (c - 1, jnp.where(cross, 1 - h, h))
        return remote(edge_s.at[n, j], edge_r.at[slot, j], e_send.at[j, n], e_recv.at[j, slot], dev)

    def edge_arrival(n, j):
        return remote(edge_s.at[n, j], edge_r.at[n, j], e_send.at[j, n], e_recv.at[j, n], prv)

    def x_copy(i, r, j):
        return remote(xs.at[i, r, j], xr.at[i, r, j], x_send.at[i, r, j], x_recv.at[i, r, j], partner)

    def dq_copy(n):
        return pltpu.make_async_copy(dq_s.at[n], dq_hbm.at[:, n], dq_sem.at[n])

    def send_tail_sums(i):
        n = head_of(0, i)

        @pl.when(before_turn)
        def _():
            xs[i, 1, 0] = (ak[n, TOK:] * SCALE).astype(bf16)
            xs[i, 1, 1] = av[n, TOK:].astype(bf16)

        @pl.when(jnp.logical_not(before_turn))
        def _():
            @pl.when(has_next)
            def _():
                edge_arrival(n, 0).wait_recv()
                edge_arrival(n, 1).wait_recv()

            xs[i, 1, 0] = (ak[n, TOK:] * SCALE + edge_r[n, 0].astype(f32)).astype(bf16)
            xs[i, 1, 1] = (av[n, TOK:] + edge_r[n, 1].astype(f32)).astype(bf16)

        x_copy(i, 1, 0).start()
        x_copy(i, 1, 1).start()

    def step(s, _):
        i = lax.rem(s, HALF)
        late = lax.rem(s // HALF, 2)
        grp = s // (2 * HALF)
        n = head_of(grp, i)
        crossing = late + par == 1
        t0 = 2 * jnp.where(late == 1, par, 1 - par)

        @pl.when(late == 0)
        def _():
            q_copy(n).wait()
            g_copy(n).wait()

        @pl.when(crossing & (i == 0) & (grp == 0))
        def _():
            @pl.when(has_prev)
            def _():
                doc_copy().wait_recv()

            doc_columns(0, doc_halo, 2)
            doc_columns(1, doc_halo, 3)
            build_mask(0)
            build_mask(1)

        @pl.when(crossing & has_prev)
        def _():
            halo_copy(n, 0).wait_recv()
            halo_copy(n, 1).wait_recv()

        res = []
        for j in range(2):
            t = t0 + j
            rows = pl.ds(pl.multiple_of(t * 256, 256), 256)
            keys = pl.ds(pl.multiple_of(t * 128, 128), 384)
            q = q_raw.at[n].reshape(1024, 128)[rows, :]
            g = g_raw.at[n].reshape(1024, 128)[rows, :]
            dq, dk, dv = attention_tile(q, g, kt[n, keys], vt[n, keys], mask[t], onehot[...])
            dq_s.at[n].reshape(1024, 128)[rows, :] = dq
            res.append((dk, dv))
        base = pl.ds(pl.multiple_of(t0 * 128, 128), TOK)
        for acc, x, y in ((ak, res[0][0], res[1][0]), (av, res[0][1], res[1][1])):
            acc[n, base] += jnp.concatenate([x[:128], x[128:] + y[:256], y[256:]], 0)

        @pl.when(crossing & has_prev)
        def _():
            edge_s[n, 0] = (ak[n, :WINDOW] * SCALE).astype(bf16)
            edge_s[n, 1] = av[n, :WINDOW].astype(bf16)
            edge_copy(n, 0).start()
            edge_copy(n, 1).start()

        @pl.when(late == 1)
        def _():
            dq_copy(n).start()

        @pl.when((late == 1) & (grp == 0))
        def _():
            xs[i, 0, 0] = (ak[n, WINDOW:TOK] * SCALE).astype(bf16)
            xs[i, 0, 1] = av[n, WINDOW:TOK].astype(bf16)
            x_copy(i, 0, 0).start()
            x_copy(i, 0, 1).start()

        @pl.when((par == 0) & (s >= 1) & (s <= HALF))
        def _():
            send_tail_sums(s - 1)

        @pl.when((par == 1) & (s >= 2 * HALF) & (s < 3 * HALF))
        def _():
            send_tail_sums(s - 2 * HALF)

        return 0

    lax.fori_loop(0, 4 * HALF, step, 0)

    def out_copy(j, r):
        src, dst = ((out_k, dk_hbm), (out_v, dv_hbm))[j]
        rows = pl.ds(r * WINDOW, WINDOW)
        return pltpu.make_async_copy(src.at[rows], dst.at[rows], out_sem.at[j, r])

    def finish(r):
        def wait_head(i, _):
            x_copy(i, r, 0).wait_recv()
            x_copy(i, r, 1).wait_recv()
            if r == 1:

                @pl.when(has_next)
                def _():
                    edge_arrival(HALF * h + i, 0).wait_recv()
                    edge_arrival(HALF * h + i, 1).wait_recv()

                @pl.when(before_turn)
                def _():
                    n, slot = head_of(1, i), head_of(0, i)
                    edge_arrival(slot, 0).wait_recv()
                    edge_arrival(slot, 1).wait_recv()
                    ak[n, TOK:] += edge_r[slot, 0].astype(f32) * (1.0 / SCALE)
                    av[n, TOK:] += edge_r[slot, 1].astype(f32)

            return 0

        lax.fori_loop(0, HALF, wait_head, 0)
        own = pl.ds(HALF * h, HALF)

        def body(b, _):
            t = pl.multiple_of(b * 32, 32)
            part = pl.ds(t, 32)
            accs = pl.ds(pl.multiple_of((r + 1) * WINDOW + t, 32), 32)
            outs = pl.ds(pl.multiple_of(r * WINDOW + t, 32), 32)
            for j, acc, scale, out in ((0, ak, SCALE, out_k), (1, av, None, out_v)):
                val = acc[own, accs]
                if scale is not None:
                    val = val * scale
                val = val + xr[:, r, j, part].astype(f32)
                if r == 1:
                    val = val + edge_r[own, j, part].astype(f32)
                out[outs] = jnp.swapaxes(val.astype(bf16), 0, 1)
            return 0

        lax.fori_loop(0, WINDOW // 32, body, 0)
        out_copy(0, r).start()
        out_copy(1, r).start()

    @pl.when(par == 0)
    def _():
        finish(1)
        finish(0)

    @pl.when(par == 1)
    def _():
        finish(0)
        finish(1)

    @pl.when(has_next)
    def _():
        doc_copy().wait_send()

    def drain(n, _):
        @pl.when(has_next)
        def _():
            halo_copy(n, 0).wait_send()
            halo_copy(n, 1).wait_send()

        @pl.when(has_prev)
        def _():
            edge_copy(n, 0).wait_send()
            edge_copy(n, 1).wait_send()

        dq_copy(n).wait()
        return 0

    lax.fori_loop(0, KV, drain, 0)

    def drain_x(i, _):
        for r in range(2):
            for j in range(2):
                x_copy(i, r, j).wait_send()
        return 0

    lax.fori_loop(0, HALF, drain_x, 0)
    for r in range(2):
        for j in range(2):
            out_copy(j, r).wait()


def deliver(dq_in, dk_in, dv_in, dq_out, dk_out, dv_out, sem):
    copies = []
    for j in range(PIECES):
        rows = pl.ds(j * (TOK // PIECES), TOK // PIECES)
        for a, (src, dst) in enumerate(((dq_in, dq_out), (dk_in, dk_out), (dv_in, dv_out))):
            copies.append(pltpu.make_async_copy(src.at[rows], dst.at[rows], sem.at[a, j]))
    for copy in copies:
        copy.start()
    for copy in copies:
        copy.wait()


def on_device(queries, key_heads, value_heads, out_grad, doc_ids):
    hbm = pl.BlockSpec(memory_space=pl.ANY)
    vmem = pl.BlockSpec(memory_space=pltpu.VMEM)
    dma = pltpu.SemaphoreType.DMA
    parts = pl.pallas_call(
        kernel,
        out_shape=(
            jax.ShapeDtypeStruct((TOK, KV, 2, HD), bf16),
            jax.ShapeDtypeStruct((TOK, HALF, HD), bf16),
            jax.ShapeDtypeStruct((TOK, HALF, HD), bf16),
        ),
        in_specs=[hbm, hbm, hbm, hbm, vmem],
        out_specs=(hbm, hbm, hbm),
        scratch_shapes=[
            pltpu.VMEM((KV, TOK, 2, HD), bf16),
            pltpu.VMEM((KV, TOK, 2, HD), bf16),
            pltpu.VMEM((TOK, KV, HD), bf16),
            pltpu.VMEM((TOK, KV, HD), bf16),
            pltpu.VMEM((KV, TOK + WINDOW, HD), bf16),
            pltpu.VMEM((KV, TOK + WINDOW, HD), bf16),
            pltpu.VMEM((4, 384, HD), bf16),
            pltpu.VMEM((256, HD), bf16),
            pltpu.VMEM((4, 128), jnp.int32),
            pltpu.VMEM((6, 128, 128), f32),
            pltpu.VMEM((KV, TOK, 2, HD), bf16),
            pltpu.VMEM((KV, TOK + WINDOW, HD), f32),
            pltpu.VMEM((KV, TOK + WINDOW, HD), f32),
            pltpu.VMEM((KV, 2, WINDOW, HD), bf16),
            pltpu.VMEM((KV, 2, WINDOW, HD), bf16),
            pltpu.VMEM((HALF, 2, 2, WINDOW, HD), bf16),
            pltpu.VMEM((HALF, 2, 2, WINDOW, HD), bf16),
            pltpu.VMEM((TOK, HALF, HD), bf16),
            pltpu.VMEM((TOK, HALF, HD), bf16),
            dma((2, KV)),
            dma((2, 2)),
            dma((2, KV)),
            dma((2, KV)),
            dma(()),
            dma(()),
            dma((2, KV)),
            dma((2, KV)),
            dma((HALF, 2, 2)),
            dma((HALF, 2, 2)),
            dma((KV,)),
            dma((2, 2)),
        ],
        compiler_params=pltpu.CompilerParams(
            collective_id=0, has_side_effects=True, vmem_limit_bytes=56 * 1024 * 1024
        ),
        cost_estimate=pl.CostEstimate(flops=8 * 10**9, bytes_accessed=9 * 2**20, transcendentals=3 * 10**6),
    )(queries, key_heads, value_heads, out_grad, doc_ids.reshape(4, 128))
    return pl.pallas_call(
        deliver,
        out_shape=tuple(jax.ShapeDtypeStruct(p.shape, p.dtype) for p in parts),
        in_specs=[hbm] * 3,
        out_specs=(hbm,) * 3,
        scratch_shapes=[dma((3, PIECES))],
        compiler_params=pltpu.CompilerParams(vmem_limit_bytes=56 * 1024 * 1024),
    )(*parts)


def solution(mesh):
    return jax.shard_map(
        on_device,
        mesh=mesh,
        in_specs=(
            P("ctx", None, "head", None),
            P("ctx", None, None),
            P("ctx", None, None),
            P("ctx", None, "head", None),
            P("ctx"),
        ),
        out_specs=(P("ctx", None, "head", None), P("ctx", "head", None), P("ctx", "head", None)),
        check_vma=False,
    )
```

```python
import functools

import jax
import jax.numpy as jnp
from jax import lax
from jax.experimental import pallas as pl
from jax.experimental.pallas import tpu as pltpu
from jax.sharding import PartitionSpec as P

MESH = pl.DeviceIdType.MESH
WINDOW = 256
TOK = 512
KV = 8
HD = 128
HALF = 4
NCTX = 128
TURN = NCTX // 2
SCALE = HD**-0.5
EXP_SCALE = SCALE * 1.4426950408889634
HIDDEN = -1e30
PIECES = 4
CHUNK = 128
NT = (((1,), (1,)), ((), ()))
NN = (((1,), (0,)), ((), ()))
TN = (((0,), (0,)), ((), ()))
bf16 = jnp.bfloat16
f32 = jnp.float32


def dot(a, b, dims):
    return lax.dot_general(a, b, dims, preferred_element_type=f32)


def kernel(
    q_hbm, k_hbm, v_hbm, g_hbm, doc_ref,
    dq_hbm, dk_hbm, dv_hbm,
    q_raw, g_raw, k_raw, v_raw, qt, gt, kt, vt, mask, onehot, doc_halo, doc_col,
    dqt, dq_s, ak, av, edge_s, edge_r, xs, xr, out_k, out_v,
    s_a, s_b, dp_a, dp_b, p_a, p_b, ds_a, ds_b,
    in_sem, kv_sem, f_send, f_recv, d_send, d_recv, e_send, e_recv, x_send, x_recv, dq_sem, out_sem,
):
    c = lax.axis_index("ctx")
    h = lax.axis_index("head")
    par = lax.rem(c, 2)
    first, last = c == 0, c == NCTX - 1
    has_prev, has_next = c > 0, c < NCTX - 1
    before_turn, after_turn = c == TURN - 1, c == TURN
    partner, nxt, prv = (c, 1 - h), (c + 1, h), (c - 1, h)
    nxt_v = (c + 1, jnp.where(before_turn, 1 - h, h))

    def remote(src, dst, send, recv, dev):
        return pltpu.make_async_remote_copy(
            src_ref=src, dst_ref=dst, send_sem=send, recv_sem=recv, device_id=dev, device_id_type=MESH
        )

    def head_of(grp, i):
        return HALF * jnp.where(grp == 0, 1 - h, h) + i

    barrier = pltpu.get_barrier_semaphore()
    pl.semaphore_signal(barrier, inc=1, device_id=partner, device_id_type=MESH)

    @pl.when(has_prev)
    def _():
        pl.semaphore_signal(barrier, inc=1, device_id=prv, device_id_type=MESH)

    @pl.when(par == 0)
    def _():
        pl.semaphore_signal(barrier, inc=1, device_id=nxt, device_id_type=MESH)

    @pl.when(after_turn)
    def _():
        pl.semaphore_signal(barrier, inc=1, device_id=(c - 1, 1 - h), device_id_type=MESH)

    def kv_copy(j, r):
        src, dst = ((k_hbm, k_raw), (v_hbm, v_raw))[j]
        rows = pl.ds(r * WINDOW, WINDOW)
        return pltpu.make_async_copy(src.at[rows], dst.at[rows], kv_sem.at[j, r])

    def qg_copy(j, part):
        src, dst = ((q_hbm, q_raw), (g_hbm, g_raw))[j]
        return pltpu.make_async_copy(src.at[:, part], dst.at[part], in_sem.at[j, part])

    for j in (0, 1):
        kv_copy(j, 1).start()
    for j in (0, 1):
        kv_copy(j, 0).start()
    for part in (1 - h, h):
        for j in (0, 1):
            qg_copy(j, part).start()

    def clear(n, _):
        ak[n] = jnp.zeros((TOK + WINDOW, HD), f32)
        av[n] = jnp.zeros((TOK + WINDOW, HD), f32)
        return 0

    lax.fori_loop(0, KV, clear, 0)

    key_row = lax.broadcasted_iota(jnp.int32, (128, 128), 0)
    tok_col = lax.broadcasted_iota(jnp.int32, (128, 128), 1)
    onehot[:128] = jnp.where(key_row == tok_col, 1.0, 0.0).astype(bf16)
    onehot[128:] = jnp.where(key_row == tok_col, 1.0, 0.0).astype(bf16)
    p_b[...] = jnp.zeros(p_b.shape, bf16)
    ds_b[...] = jnp.zeros(ds_b.shape, bf16)

    @pl.when(first)
    def _():
        kt[:, :WINDOW] = jnp.zeros((KV, WINDOW, HD), bf16)
        vt[:, :WINDOW] = jnp.zeros((KV, WINDOW, HD), bf16)
        doc_halo[...] = jnp.full((4, 128), -1, jnp.int32)

    @pl.when(last)
    def _():
        edge_r[...] = jnp.zeros(edge_r.shape, bf16)

    def swap(src, dst, r):
        def body(b, _):
            t = pl.multiple_of(r * WINDOW + b * CHUNK, CHUNK)
            dst[:, pl.ds(pl.multiple_of(t + WINDOW, CHUNK), CHUNK)] = jnp.swapaxes(src[pl.ds(t, CHUNK)], 0, 1)
            return 0

        lax.fori_loop(0, WINDOW // CHUNK, body, 0)

    for j, src, dst in ((0, k_raw, kt), (1, v_raw, vt)):
        kv_copy(j, 1).wait()
        swap(src, dst, 1)

    def doc_copy():
        return remote(doc_ref, doc_halo, d_send, d_recv, nxt)

    def halo_copy(n, j):
        ref = (kt, vt)[j]
        dev = (nxt, nxt_v)[j]
        return remote(
            ref.at[n, pl.ds(TOK, WINDOW)], ref.at[n, pl.ds(0, WINDOW)], f_send.at[j, n], f_recv.at[j, n], dev
        )

    @pl.when(par == 0)
    def _():
        pl.semaphore_wait(barrier, 2)

    @pl.when((par == 1) & has_next & jnp.logical_not(before_turn))
    def _():
        pl.semaphore_wait(barrier, 3)

    @pl.when(before_turn)
    def _():
        pl.semaphore_wait(barrier, 4)

    @pl.when(last)
    def _():
        pl.semaphore_wait(barrier, 2)

    @pl.when(has_next)
    def _():
        doc_copy().start()

        def send_halo(i, _):
            n = head_of(i // HALF, lax.rem(i, HALF))
            halo_copy(n, 0).start()
            halo_copy(jnp.where(before_turn, lax.rem(n + HALF, KV), n), 1).start()
            return 0

        lax.fori_loop(0, KV, send_halo, 0)

    for j, src, dst in ((0, k_raw, kt), (1, v_raw, vt)):
        kv_copy(j, 0).wait()
        swap(src, dst, 0)

    def doc_columns(block, ref, r):
        wide = jnp.broadcast_to(ref[r : r + 1, :], (128, 128)).astype(f32)
        doc_col[block] = wide.T

    def build_mask(t):
        docs = jnp.broadcast_to(doc_ref[t : t + 1, :], (128, 128)).astype(f32)
        for b, inside in enumerate((key_row > tok_col, None, key_row <= tok_col)):
            same = doc_col[t + b] == docs
            seen = same if inside is None else same & inside
            mask[t, b * 128 : (b + 1) * 128] = jnp.where(seen, 0.0, HIDDEN).astype(bf16)

    for b in range(4):
        doc_columns(2 + b, doc_ref, b)
    build_mask(2)
    build_mask(3)

    def edge_copy(n, j):
        cross = after_turn & (n // HALF != h)
        slot = jnp.where(cross, lax.rem(n + HALF, KV), n)
        dev = (c - 1, jnp.where(cross, 1 - h, h))
        return remote(edge_s.at[n, j], edge_r.at[slot, j], e_send.at[j, n], e_recv.at[j, slot], dev)

    def edge_arrival(n, j):
        return remote(edge_s.at[n, j], edge_r.at[n, j], e_send.at[j, n], e_recv.at[j, n], prv)

    def x_copy(i, r, j):
        return remote(xs.at[i, r, j], xr.at[i, r, j], x_send.at[i, r, j], x_recv.at[i, r, j], partner)

    def dq_copy(part):
        return pltpu.make_async_copy(dq_s.at[part], dq_hbm.at[:, part], dq_sem.at[part])

    def swap_in(part):
        for j, src, dst in ((0, q_raw, qt), (1, g_raw, gt)):
            qg_copy(j, part).wait()

            def body(b, _, src=src, dst=dst):
                t = pl.ds(pl.multiple_of(b * CHUNK, CHUNK), CHUNK)
                dst[pl.ds(part * KV, KV), t] = jnp.swapaxes(src[part, t], 0, 1)
                return 0

            lax.fori_loop(0, TOK // CHUNK, body, 0)

    def swap_out(part):
        def body(b, _):
            t = pl.ds(pl.multiple_of(b * CHUNK, CHUNK), CHUNK)
            dq_s[part, t] = jnp.swapaxes(dqt[pl.ds(part * KV, KV), t], 0, 1)
            return 0

        lax.fori_loop(0, TOK // CHUNK, body, 0)
        dq_copy(part).start()

    def send_tail_sums(i):
        n = head_of(0, i)

        @pl.when(before_turn)
        def _():
            xs[i, 1, 0] = (ak[n, TOK:] * SCALE).astype(bf16)
            xs[i, 1, 1] = av[n, TOK:].astype(bf16)

        @pl.when(jnp.logical_not(before_turn))
        def _():
            @pl.when(has_next)
            def _():
                edge_arrival(n, 0).wait_recv()
                edge_arrival(n, 1).wait_recv()

            xs[i, 1, 0] = (ak[n, TOK:] * SCALE + edge_r[n, 0].astype(f32)).astype(bf16)
            xs[i, 1, 1] = (av[n, TOK:] + edge_r[n, 1].astype(f32)).astype(bf16)

        x_copy(i, 1, 0).start()
        x_copy(i, 1, 1).start()

    def plan(s):
        i = lax.rem(s, HALF)
        grp = s // (2 * HALF)
        late = lax.rem(s // HALF + jnp.where((grp == 1) & (par == 0), 1, 0), 2)
        t0 = 2 * jnp.where(late == 1, par, 1 - par)
        return i, late, grp, head_of(grp, i), t0, late + par == 1

    def places(n, t0, j):
        t = t0 + j
        toks = pl.ds(pl.multiple_of(t * 128, 128), 128)
        keys = pl.ds(pl.multiple_of(t * 128, 128), 384)
        return t, (pl.ds(2 * n, 2), toks), keys

    def prepare(s):
        i, _, grp, n, _, crossing = plan(s)

        @pl.when(s == 2 * HALF)
        def _():
            swap_in(h)

        @pl.when(crossing & (i == 0) & (grp == 0))
        def _():
            @pl.when(has_prev)
            def _():
                doc_copy().wait_recv()

            doc_columns(0, doc_halo, 2)
            doc_columns(1, doc_halo, 3)
            build_mask(0)
            build_mask(1)

        @pl.when(crossing & has_prev)
        def _():
            halo_copy(n, 0).wait_recv()
            halo_copy(n, 1).wait_recv()

    def front(s, s_to, dp_to):
        _, _, _, n, t0, _ = plan(s)
        for j in range(2):
            t, where, keys = places(n, t0, j)
            q = qt[where].reshape(256, HD)
            s_to[j] = dot(jnp.concatenate([kt[n, keys], mask[t]], 1), jnp.concatenate([q, onehot[...]], 1), NT)
            yield
            dp_to[j] = dot(vt[n, keys], gt[where].reshape(256, HD), NT)
            yield

    def middle(s_of, dp_of, p_to, ds_to):
        for j in range(2):
            for part in (slice(0, 128), slice(128, 256)):
                scores = s_of[j, :, part]
                dp = dp_of[j, :, part]
                top = jnp.max(scores, 0, keepdims=True)
                e = jnp.exp2((scores - top) * EXP_SCALE)
                total = jnp.sum(e, 0, keepdims=True)
                moment = jnp.sum(e * dp, 0, keepdims=True)
                inv = 1.0 / total
                p = e * inv
                ds_to[j, :, part] = (p * (dp - moment * inv)).astype(bf16)
                p_to[j, :, part] = p.astype(bf16)
                yield

    def back(s, p_of, ds_of):
        _, _, _, n, t0, _ = plan(s)
        for j in range(2):
            _, where, keys = places(n, t0, j)
            ds = ds_of[j]
            ak[n, keys] += dot(ds, qt[where].reshape(256, HD), NN)
            av[n, keys] += dot(p_of[j], gt[where].reshape(256, HD), NN)
            yield
            dq = (dot(kt[n, keys], ds, TN) * SCALE).T.astype(bf16)
            dqt[where] = dq.reshape(2, 128, HD)
            yield

    def weave(*works):
        works = list(works)
        while works:
            works = [w for w in works if next(w, True) is None]

    def pass_on(s):
        i, late, grp, n, _, crossing = plan(s)

        @pl.when(crossing & has_prev)
        def _():
            edge_s[n, 0] = (ak[n, :WINDOW] * SCALE).astype(bf16)
            edge_s[n, 1] = av[n, :WINDOW].astype(bf16)
            edge_copy(n, 0).start()
            edge_copy(n, 1).start()

        @pl.when((late == 1) & (grp == 0))
        def _():
            xs[i, 0, 0] = (ak[n, WINDOW:TOK] * SCALE).astype(bf16)
            xs[i, 0, 1] = av[n, WINDOW:TOK].astype(bf16)
            x_copy(i, 0, 0).start()
            x_copy(i, 0, 1).start()

        @pl.when((par == 0) & (s >= 1) & (s <= HALF))
        def _():
            send_tail_sums(s - 1)

        @pl.when((par == 1) & (s >= 2 * HALF) & (s < 3 * HALF))
        def _():
            send_tail_sums(s - 2 * HALF)

        @pl.when(s == 2 * HALF - 1)
        def _():
            swap_out(1 - h)

    steps = 4 * HALF
    slots = ((s_a, dp_a, p_a, ds_a), (s_b, dp_b, p_b, ds_b))
    swap_in(1 - h)
    prepare(0)
    weave(front(0, s_a, dp_a))

    def pair(at, _):
        for k in range(2):
            s = 2 * at + k
            here, other = slots[k], slots[1 - k]

            @pl.when(s + 1 < steps)
            def _():
                prepare(s + 1)

            weave(
                middle(*here),
                back(jnp.maximum(s - 1, 0), other[2], other[3]),
                front(jnp.minimum(s + 1, steps - 1), other[0], other[1]),
            )

            @pl.when(s >= 1)
            def _():
                pass_on(s - 1)

        return 0

    lax.fori_loop(0, steps // 2, pair, 0)
    weave(back(steps - 1, p_b, ds_b))
    pass_on(steps - 1)
    swap_out(h)

    def out_copy(j, r):
        src, dst = ((out_k, dk_hbm), (out_v, dv_hbm))[j]
        rows = pl.ds(r * WINDOW, WINDOW)
        return pltpu.make_async_copy(src.at[rows], dst.at[rows], out_sem.at[j, r])

    def finish(r):
        def wait_head(i, _):
            x_copy(i, r, 0).wait_recv()
            x_copy(i, r, 1).wait_recv()
            if r == 1:

                @pl.when(has_next)
                def _():
                    edge_arrival(HALF * h + i, 0).wait_recv()
                    edge_arrival(HALF * h + i, 1).wait_recv()

                @pl.when(before_turn)
                def _():
                    n, slot = head_of(1, i), head_of(0, i)
                    edge_arrival(slot, 0).wait_recv()
                    edge_arrival(slot, 1).wait_recv()
                    ak[n, TOK:] += edge_r[slot, 0].astype(f32) * (1.0 / SCALE)
                    av[n, TOK:] += edge_r[slot, 1].astype(f32)

            return 0

        lax.fori_loop(0, HALF, wait_head, 0)
        own = pl.ds(HALF * h, HALF)

        def body(b, _):
            t = pl.multiple_of(b * CHUNK, CHUNK)
            part = pl.ds(t, CHUNK)
            accs = pl.ds(pl.multiple_of((r + 1) * WINDOW + t, CHUNK), CHUNK)
            outs = pl.ds(pl.multiple_of(r * WINDOW + t, CHUNK), CHUNK)
            for j, acc, scale, out in ((0, ak, SCALE, out_k), (1, av, None, out_v)):
                val = acc[own, accs]
                if scale is not None:
                    val = val * scale
                val = val + xr[:, r, j, part].astype(f32)
                if r == 1:
                    val = val + edge_r[own, j, part].astype(f32)
                out[outs] = jnp.swapaxes(val.astype(bf16), 0, 1)
            return 0

        lax.fori_loop(0, WINDOW // CHUNK, body, 0)
        out_copy(0, r).start()
        out_copy(1, r).start()

    @pl.when(par == 0)
    def _():
        finish(1)
        finish(0)

    @pl.when(par == 1)
    def _():
        finish(0)
        finish(1)

    @pl.when(has_next)
    def _():
        doc_copy().wait_send()

    def drain(n, _):
        @pl.when(has_next)
        def _():
            halo_copy(n, 0).wait_send()
            halo_copy(n, 1).wait_send()

        @pl.when(has_prev)
        def _():
            edge_copy(n, 0).wait_send()
            edge_copy(n, 1).wait_send()

        return 0

    lax.fori_loop(0, KV, drain, 0)
    for part in range(2):
        dq_copy(part).wait()

    def drain_x(i, _):
        for r in range(2):
            for j in range(2):
                x_copy(i, r, j).wait_send()
        return 0

    lax.fori_loop(0, HALF, drain_x, 0)
    for r in range(2):
        for j in range(2):
            out_copy(j, r).wait()


def deliver(dq_in, dk_in, dv_in, dq_out, dk_out, dv_out, dq_v, dk_v, dv_v, in_sem, out_sem):
    ways = ((dq_in, dq_v, dq_out), (dk_in, dk_v, dk_out), (dv_in, dv_v, dv_out))
    moves = []
    for j in range(PIECES):
        rows = pl.ds(j * (TOK // PIECES), TOK // PIECES)
        for a, (src, mid, dst) in enumerate(ways):
            moves.append((
                pltpu.make_async_copy(src.at[rows], mid.at[rows], in_sem.at[a, j]),
                pltpu.make_async_copy(mid.at[rows], dst.at[rows], out_sem.at[a, j]),
            ))
    for load, _ in moves:
        load.start()
    for load, store in moves:
        load.wait()
        store.start()
    for _, store in moves:
        store.wait()


def on_device(queries, key_heads, value_heads, out_grad, doc_ids):
    hbm = pl.BlockSpec(memory_space=pl.ANY)
    vmem = pl.BlockSpec(memory_space=pltpu.VMEM)
    dma = pltpu.SemaphoreType.DMA
    parts = pl.pallas_call(
        kernel,
        out_shape=(
            jax.ShapeDtypeStruct((TOK, 2, KV, HD), bf16),
            jax.ShapeDtypeStruct((TOK, HALF, HD), bf16),
            jax.ShapeDtypeStruct((TOK, HALF, HD), bf16),
        ),
        in_specs=[hbm, hbm, hbm, hbm, vmem],
        out_specs=(hbm, hbm, hbm),
        scratch_shapes=[
            pltpu.VMEM((2, TOK, KV, HD), bf16),
            pltpu.VMEM((2, TOK, KV, HD), bf16),
            pltpu.VMEM((TOK, KV, HD), bf16),
            pltpu.VMEM((TOK, KV, HD), bf16),
            pltpu.VMEM((2 * KV, TOK, HD), bf16),
            pltpu.VMEM((2 * KV, TOK, HD), bf16),
            pltpu.VMEM((KV, TOK + WINDOW, HD), bf16),
            pltpu.VMEM((KV, TOK + WINDOW, HD), bf16),
            pltpu.VMEM((4, 384, HD), bf16),
            pltpu.VMEM((256, HD), bf16),
            pltpu.VMEM((4, 128), jnp.int32),
            pltpu.VMEM((6, 128, 128), f32),
            pltpu.VMEM((2 * KV, TOK, HD), bf16),
            pltpu.VMEM((2, TOK, KV, HD), bf16),
            pltpu.VMEM((KV, TOK + WINDOW, HD), f32),
            pltpu.VMEM((KV, TOK + WINDOW, HD), f32),
            pltpu.VMEM((KV, 2, WINDOW, HD), bf16),
            pltpu.VMEM((KV, 2, WINDOW, HD), bf16),
            pltpu.VMEM((HALF, 2, 2, WINDOW, HD), bf16),
            pltpu.VMEM((HALF, 2, 2, WINDOW, HD), bf16),
            pltpu.VMEM((TOK, HALF, HD), bf16),
            pltpu.VMEM((TOK, HALF, HD), bf16),
            pltpu.VMEM((2, 384, 256), f32),
            pltpu.VMEM((2, 384, 256), f32),
            pltpu.VMEM((2, 384, 256), f32),
            pltpu.VMEM((2, 384, 256), f32),
            pltpu.VMEM((2, 384, 256), bf16),
            pltpu.VMEM((2, 384, 256), bf16),
            pltpu.VMEM((2, 384, 256), bf16),
            pltpu.VMEM((2, 384, 256), bf16),
            dma((2, 2)),
            dma((2, 2)),
            dma((2, KV)),
            dma((2, KV)),
            dma(()),
            dma(()),
            dma((2, KV)),
            dma((2, KV)),
            dma((HALF, 2, 2)),
            dma((HALF, 2, 2)),
            dma((2,)),
            dma((2, 2)),
        ],
        compiler_params=pltpu.CompilerParams(
            collective_id=0, has_side_effects=True, vmem_limit_bytes=56 * 1024 * 1024
        ),
        cost_estimate=pl.CostEstimate(flops=8 * 10**9, bytes_accessed=9 * 2**20, transcendentals=3 * 10**6),
    )(
        queries.reshape(TOK, 2, KV, HD), key_heads, value_heads, out_grad.reshape(TOK, 2, KV, HD),
        doc_ids.reshape(4, 128),
    )
    query_grad, key_grad, value_grad = pl.pallas_call(
        deliver,
        out_shape=tuple(jax.ShapeDtypeStruct(p.shape, p.dtype) for p in parts),
        in_specs=[hbm] * 3,
        out_specs=(hbm,) * 3,
        scratch_shapes=[pltpu.VMEM(p.shape, p.dtype) for p in parts] + [dma((3, PIECES)), dma((3, PIECES))],
        compiler_params=pltpu.CompilerParams(vmem_limit_bytes=56 * 1024 * 1024),
    )(*parts)
    return query_grad.reshape(TOK, KV, 2, HD), key_grad, value_grad


def solution(mesh):
    return jax.shard_map(
        on_device,
        mesh=mesh,
        in_specs=(
            P("ctx", None, "head", None),
            P("ctx", None, None),
            P("ctx", None, None),
            P("ctx", None, "head", None),
            P("ctx"),
        ),
        out_specs=(P("ctx", None, "head", None), P("ctx", "head", None), P("ctx", "head", None)),
        check_vma=False,
    )
```

```python
import functools

import jax
import jax.numpy as jnp
from jax import lax
from jax.experimental import pallas as pl
from jax.experimental.pallas import tpu as pltpu
from jax.sharding import PartitionSpec as P

MESH = pl.DeviceIdType.MESH
WINDOW = 256
TOK = 512
KV = 8
HD = 128
HALF = 4
NCTX = 128
TURN = NCTX // 2
SCALE = HD**-0.5
EXP_SCALE = SCALE * 1.4426950408889634
HIDDEN = -1e30
PIECES = 2
CHUNK = 128
NT = (((1,), (1,)), ((), ()))
NN = (((1,), (0,)), ((), ()))
TN = (((0,), (0,)), ((), ()))
bf16 = jnp.bfloat16
f32 = jnp.float32


def dot(a, b, dims):
    return lax.dot_general(a, b, dims, preferred_element_type=f32)


def kernel(
    q_hbm, k_hbm, v_hbm, g_hbm, doc_ref,
    dq_hbm, dk_hbm, dv_hbm,
    q_raw, g_raw, k_raw, v_raw, qt, gt, kt, vt, mask, onehot, doc_halo, doc_col,
    dqt, dq_s, ak, av, edge_s, edge_r, xs, xr, out_k, out_v,
    s_a, s_b, dp_a, dp_b, p_a, p_b, ds_a, ds_b,
    in_sem, kv_sem, f_send, f_recv, d_send, d_recv, e_send, e_recv, x_send, x_recv, dq_sem, out_sem,
):
    c = lax.axis_index("ctx")
    h = lax.axis_index("head")
    par = lax.rem(c, 2)
    first, last = c == 0, c == NCTX - 1
    has_prev, has_next = c > 0, c < NCTX - 1
    before_turn, after_turn = c == TURN - 1, c == TURN
    partner, nxt, prv = (c, 1 - h), (c + 1, h), (c - 1, h)
    nxt_v = (c + 1, jnp.where(before_turn, 1 - h, h))

    def remote(src, dst, send, recv, dev):
        return pltpu.make_async_remote_copy(
            src_ref=src, dst_ref=dst, send_sem=send, recv_sem=recv, device_id=dev, device_id_type=MESH
        )

    def head_of(grp, i):
        return HALF * jnp.where(grp == 0, 1 - h, h) + i

    barrier = pltpu.get_barrier_semaphore()
    pl.semaphore_signal(barrier, inc=1, device_id=partner, device_id_type=MESH)

    @pl.when(has_prev)
    def _():
        pl.semaphore_signal(barrier, inc=1, device_id=prv, device_id_type=MESH)

    @pl.when(par == 0)
    def _():
        pl.semaphore_signal(barrier, inc=1, device_id=nxt, device_id_type=MESH)

    @pl.when(after_turn)
    def _():
        pl.semaphore_signal(barrier, inc=1, device_id=(c - 1, 1 - h), device_id_type=MESH)

    def kv_copy(j, r):
        src, dst = ((k_hbm, k_raw), (v_hbm, v_raw))[j]
        rows = pl.ds(r * WINDOW, WINDOW)
        return pltpu.make_async_copy(src.at[rows], dst.at[rows], kv_sem.at[j, r])

    def qg_copy(j, part):
        src, dst = ((q_hbm, q_raw), (g_hbm, g_raw))[j]
        return pltpu.make_async_copy(src.at[:, part], dst.at[part], in_sem.at[j, part])

    for j in (0, 1):
        kv_copy(j, 1).start()
    for j in (0, 1):
        kv_copy(j, 0).start()
    for part in (1 - h, h):
        for j in (0, 1):
            qg_copy(j, part).start()

    def clear(n, _):
        ak[n] = jnp.zeros((TOK + WINDOW, HD), f32)
        av[n] = jnp.zeros((TOK + WINDOW, HD), f32)
        return 0

    lax.fori_loop(0, KV, clear, 0)

    key_row = lax.broadcasted_iota(jnp.int32, (128, 128), 0)
    tok_col = lax.broadcasted_iota(jnp.int32, (128, 128), 1)
    onehot[:128] = jnp.where(key_row == tok_col, 1.0, 0.0).astype(bf16)
    onehot[128:] = jnp.where(key_row == tok_col, 1.0, 0.0).astype(bf16)
    p_b[...] = jnp.zeros(p_b.shape, bf16)
    ds_b[...] = jnp.zeros(ds_b.shape, bf16)

    @pl.when(first)
    def _():
        kt[:, :WINDOW] = jnp.zeros((KV, WINDOW, HD), bf16)
        vt[:, :WINDOW] = jnp.zeros((KV, WINDOW, HD), bf16)
        doc_halo[...] = jnp.full((4, 128), -1, jnp.int32)

    @pl.when(last)
    def _():
        edge_r[...] = jnp.zeros(edge_r.shape, bf16)

    def swap(src, dst, r):
        def body(b, _):
            t = pl.multiple_of(r * WINDOW + b * CHUNK, CHUNK)
            dst[:, pl.ds(pl.multiple_of(t + WINDOW, CHUNK), CHUNK)] = jnp.swapaxes(src[pl.ds(t, CHUNK)], 0, 1)
            return 0

        lax.fori_loop(0, WINDOW // CHUNK, body, 0)

    for j, src, dst in ((0, k_raw, kt), (1, v_raw, vt)):
        kv_copy(j, 1).wait()
        swap(src, dst, 1)

    def doc_copy():
        return remote(doc_ref, doc_halo, d_send, d_recv, nxt)

    def halo_copy(n, j):
        ref = (kt, vt)[j]
        dev = (nxt, nxt_v)[j]
        return remote(
            ref.at[n, pl.ds(TOK, WINDOW)], ref.at[n, pl.ds(0, WINDOW)], f_send.at[j, n], f_recv.at[j, n], dev
        )

    @pl.when(par == 0)
    def _():
        pl.semaphore_wait(barrier, 2)

    @pl.when((par == 1) & has_next & jnp.logical_not(before_turn))
    def _():
        pl.semaphore_wait(barrier, 3)

    @pl.when(before_turn)
    def _():
        pl.semaphore_wait(barrier, 4)

    @pl.when(last)
    def _():
        pl.semaphore_wait(barrier, 2)

    def send_halo(grp):
        @pl.when(has_next)
        def _():
            def body(i, _):
                n = head_of(grp, i)
                halo_copy(n, 0).start()
                halo_copy(jnp.where(before_turn, lax.rem(n + HALF, KV), n), 1).start()
                return 0

            lax.fori_loop(0, HALF, body, 0)

    @pl.when(has_next)
    def _():
        doc_copy().start()

    send_halo(0)

    for j, src, dst in ((0, k_raw, kt), (1, v_raw, vt)):
        kv_copy(j, 0).wait()
        swap(src, dst, 0)

    def doc_columns(block, ref, r):
        wide = jnp.broadcast_to(ref[r : r + 1, :], (128, 128)).astype(f32)
        doc_col[block] = wide.T

    def build_mask(t):
        docs = jnp.broadcast_to(doc_ref[t : t + 1, :], (128, 128)).astype(f32)
        for b, inside in enumerate((key_row > tok_col, None, key_row <= tok_col)):
            same = doc_col[t + b] == docs
            seen = same if inside is None else same & inside
            mask[t, b * 128 : (b + 1) * 128] = jnp.where(seen, 0.0, HIDDEN).astype(bf16)

    for b in range(4):
        doc_columns(2 + b, doc_ref, b)
    build_mask(2)
    build_mask(3)

    def edge_copy(n):
        cross = after_turn & (n // HALF != h)
        slot = jnp.where(cross, lax.rem(n + HALF, KV), n)
        dev = (c - 1, jnp.where(cross, 1 - h, h))
        return remote(edge_s.at[n], edge_r.at[slot], e_send.at[n], e_recv.at[slot], dev)

    def edge_arrival(n):
        return remote(edge_s.at[n], edge_r.at[n], e_send.at[n], e_recv.at[n], prv)

    def x_copy(i, r):
        return remote(xs.at[i, r], xr.at[i, r], x_send.at[i, r], x_recv.at[i, r], partner)

    def dq_copy(part):
        return pltpu.make_async_copy(dq_s.at[part], dq_hbm.at[:, part], dq_sem.at[part])

    def swap_in(part):
        for j, src, dst in ((0, q_raw, qt), (1, g_raw, gt)):
            qg_copy(j, part).wait()

            def body(b, _, src=src, dst=dst):
                t = pl.ds(pl.multiple_of(b * CHUNK, CHUNK), CHUNK)
                dst[pl.ds(part * KV, KV), t] = jnp.swapaxes(src[part, t], 0, 1)
                return 0

            lax.fori_loop(0, TOK // CHUNK, body, 0)

    def swap_out(part):
        def body(b, _):
            t = pl.ds(pl.multiple_of(b * CHUNK, CHUNK), CHUNK)
            dq_s[part, t] = jnp.swapaxes(dqt[pl.ds(part * KV, KV), t], 0, 1)
            return 0

        lax.fori_loop(0, TOK // CHUNK, body, 0)
        dq_copy(part).start()

    def send_tail_sums(i):
        n = head_of(0, i)

        @pl.when(before_turn)
        def _():
            xs[i, 1, 0] = (ak[n, TOK:] * SCALE).astype(bf16)
            xs[i, 1, 1] = av[n, TOK:].astype(bf16)

        @pl.when(jnp.logical_not(before_turn))
        def _():
            @pl.when(has_next)
            def _():
                edge_arrival(n).wait_recv()

            xs[i, 1, 0] = (ak[n, TOK:] * SCALE + edge_r[n, 0].astype(f32)).astype(bf16)
            xs[i, 1, 1] = (av[n, TOK:] + edge_r[n, 1].astype(f32)).astype(bf16)

        x_copy(i, 1).start()

    def plan(s):
        i = lax.rem(s, HALF)
        grp = s // (2 * HALF)
        late = lax.rem(s // HALF + jnp.where((grp == 1) & (par == 0), 1, 0), 2)
        t0 = 2 * jnp.where(late == 1, par, 1 - par)
        return i, late, grp, head_of(grp, i), t0, late + par == 1

    def places(n, t0, j):
        t = t0 + j
        toks = pl.ds(pl.multiple_of(t * 128, 128), 128)
        keys = pl.ds(pl.multiple_of(t * 128, 128), 384)
        return t, (pl.ds(2 * n, 2), toks), keys

    def prepare(s):
        i, _, grp, n, _, crossing = plan(s)

        @pl.when(s == 2 * HALF)
        def _():
            swap_in(h)

        @pl.when(crossing & (i == 0) & (grp == 0))
        def _():
            @pl.when(has_prev)
            def _():
                doc_copy().wait_recv()

            doc_columns(0, doc_halo, 2)
            doc_columns(1, doc_halo, 3)
            build_mask(0)
            build_mask(1)

        @pl.when(crossing & has_prev)
        def _():
            halo_copy(n, 0).wait_recv()
            halo_copy(n, 1).wait_recv()

    def front(s, s_to, dp_to):
        _, _, _, n, t0, _ = plan(s)
        for j in range(2):
            t, where, keys = places(n, t0, j)
            q = qt[where].reshape(256, HD)
            s_to[j] = dot(jnp.concatenate([kt[n, keys], mask[t]], 1), jnp.concatenate([q, onehot[...]], 1), NT)
            yield
            dp_to[j] = dot(vt[n, keys], gt[where].reshape(256, HD), NT)
            yield

    def middle(s_of, dp_of, p_to, ds_to):
        for j in range(2):
            for part in (slice(0, 128), slice(128, 256)):
                scores = s_of[j, :, part]
                dp = dp_of[j, :, part]
                top = jnp.max(scores, 0, keepdims=True)
                e = jnp.exp2((scores - top) * EXP_SCALE)
                total = jnp.sum(e, 0, keepdims=True)
                moment = jnp.sum(e * dp, 0, keepdims=True)
                inv = 1.0 / total
                p = e * inv
                ds_to[j, :, part] = (p * (dp - moment * inv)).astype(bf16)
                p_to[j, :, part] = p.astype(bf16)
                yield

    def back(s, p_of, ds_of):
        _, _, _, n, t0, _ = plan(s)
        for j in range(2):
            _, where, keys = places(n, t0, j)
            ds = ds_of[j]
            ak[n, keys] += dot(ds, qt[where].reshape(256, HD), NN)
            av[n, keys] += dot(p_of[j], gt[where].reshape(256, HD), NN)
            yield
            dq = (dot(kt[n, keys], ds, TN) * SCALE).T.astype(bf16)
            dqt[where] = dq.reshape(2, 128, HD)
            yield

    def weave(*works):
        works = list(works)
        while works:
            works = [w for w in works if next(w, True) is None]

    def pass_on(s):
        i, late, grp, n, _, crossing = plan(s)

        @pl.when(crossing & has_prev)
        def _():
            edge_s[n, 0] = (ak[n, :WINDOW] * SCALE).astype(bf16)
            edge_s[n, 1] = av[n, :WINDOW].astype(bf16)
            edge_copy(n).start()

        @pl.when((late == 1) & (grp == 0))
        def _():
            xs[i, 0, 0] = (ak[n, WINDOW:TOK] * SCALE).astype(bf16)
            xs[i, 0, 1] = av[n, WINDOW:TOK].astype(bf16)
            x_copy(i, 0).start()

        @pl.when((par == 0) & (s < HALF))
        def _():
            send_tail_sums(s)

        @pl.when((par == 1) & (s >= 2 * HALF) & (s < 3 * HALF))
        def _():
            send_tail_sums(s - 2 * HALF)

        @pl.when(s == 2 * HALF - 1)
        def _():
            swap_out(1 - h)

    steps = 4 * HALF
    slots = ((s_a, dp_a, p_a, ds_a), (s_b, dp_b, p_b, ds_b))
    swap_in(1 - h)
    prepare(0)
    weave(front(0, s_a, dp_a))
    send_halo(1)

    def pair(at, _):
        for k in range(2):
            s = 2 * at + k
            here, other = slots[k], slots[1 - k]

            @pl.when(s + 1 < steps)
            def _():
                prepare(s + 1)

            weave(
                middle(*here),
                back(jnp.maximum(s - 1, 0), other[2], other[3]),
                front(jnp.minimum(s + 1, steps - 1), other[0], other[1]),
            )

            @pl.when(s >= 1)
            def _():
                pass_on(s - 1)

        return 0

    lax.fori_loop(0, steps // 2, pair, 0)
    weave(back(steps - 1, p_b, ds_b))
    pass_on(steps - 1)
    swap_out(h)

    def out_copy(j, r):
        src, dst = ((out_k, dk_hbm), (out_v, dv_hbm))[j]
        rows = pl.ds(r * WINDOW, WINDOW)
        return pltpu.make_async_copy(src.at[rows], dst.at[rows], out_sem.at[j, r])

    def finish(r):
        def wait_head(i, _):
            x_copy(i, r).wait_recv()
            if r == 1:

                @pl.when(has_next)
                def _():
                    edge_arrival(HALF * h + i).wait_recv()

                @pl.when(before_turn)
                def _():
                    n, slot = head_of(1, i), head_of(0, i)
                    edge_arrival(slot).wait_recv()
                    ak[n, TOK:] += edge_r[slot, 0].astype(f32) * (1.0 / SCALE)
                    av[n, TOK:] += edge_r[slot, 1].astype(f32)

            return 0

        lax.fori_loop(0, HALF, wait_head, 0)
        own = pl.ds(HALF * h, HALF)

        def body(b, _):
            t = pl.multiple_of(b * CHUNK, CHUNK)
            part = pl.ds(t, CHUNK)
            accs = pl.ds(pl.multiple_of((r + 1) * WINDOW + t, CHUNK), CHUNK)
            outs = pl.ds(pl.multiple_of(r * WINDOW + t, CHUNK), CHUNK)
            for j, acc, scale, out in ((0, ak, SCALE, out_k), (1, av, None, out_v)):
                val = acc[own, accs]
                if scale is not None:
                    val = val * scale
                val = val + xr[:, r, j, part].astype(f32)
                if r == 1:
                    val = val + edge_r[own, j, part].astype(f32)
                out[outs] = jnp.swapaxes(val.astype(bf16), 0, 1)
            return 0

        lax.fori_loop(0, WINDOW // CHUNK, body, 0)
        out_copy(0, r).start()
        out_copy(1, r).start()

    @pl.when(par == 0)
    def _():
        finish(1)
        finish(0)

    @pl.when(par == 1)
    def _():
        finish(0)
        finish(1)

    @pl.when(has_next)
    def _():
        doc_copy().wait_send()

    def drain(n, _):
        @pl.when(has_next)
        def _():
            halo_copy(n, 0).wait_send()
            halo_copy(n, 1).wait_send()

        @pl.when(has_prev)
        def _():
            edge_copy(n).wait_send()

        return 0

    lax.fori_loop(0, KV, drain, 0)
    for part in range(2):
        dq_copy(part).wait()

    def drain_x(i, _):
        for r in range(2):
            x_copy(i, r).wait_send()
        return 0

    lax.fori_loop(0, HALF, drain_x, 0)
    for r in range(2):
        for j in range(2):
            out_copy(j, r).wait()


def deliver(dq_in, dk_in, dv_in, dq_out, dk_out, dv_out, dq_v, dk_v, dv_v, in_sem, out_sem):
    ways = ((dq_in, dq_v, dq_out), (dk_in, dk_v, dk_out), (dv_in, dv_v, dv_out))
    moves = []
    for j in range(PIECES):
        rows = pl.ds(j * (TOK // PIECES), TOK // PIECES)
        for a, (src, mid, dst) in enumerate(ways):
            moves.append((
                pltpu.make_async_copy(src.at[rows], mid.at[rows], in_sem.at[a, j]),
                pltpu.make_async_copy(mid.at[rows], dst.at[rows], out_sem.at[a, j]),
            ))
    for load, _ in moves:
        load.start()
    for load, store in moves:
        load.wait()
        store.start()
    for _, store in moves:
        store.wait()


def on_device(queries, key_heads, value_heads, out_grad, doc_ids):
    hbm = pl.BlockSpec(memory_space=pl.ANY)
    vmem = pl.BlockSpec(memory_space=pltpu.VMEM)
    dma = pltpu.SemaphoreType.DMA
    parts = pl.pallas_call(
        kernel,
        out_shape=(
            jax.ShapeDtypeStruct((TOK, 2, KV, HD), bf16),
            jax.ShapeDtypeStruct((TOK, HALF, HD), bf16),
            jax.ShapeDtypeStruct((TOK, HALF, HD), bf16),
        ),
        in_specs=[hbm, hbm, hbm, hbm, vmem],
        out_specs=(hbm, hbm, hbm),
        scratch_shapes=[
            pltpu.VMEM((2, TOK, KV, HD), bf16),
            pltpu.VMEM((2, TOK, KV, HD), bf16),
            pltpu.VMEM((TOK, KV, HD), bf16),
            pltpu.VMEM((TOK, KV, HD), bf16),
            pltpu.VMEM((2 * KV, TOK, HD), bf16),
            pltpu.VMEM((2 * KV, TOK, HD), bf16),
            pltpu.VMEM((KV, TOK + WINDOW, HD), bf16),
            pltpu.VMEM((KV, TOK + WINDOW, HD), bf16),
            pltpu.VMEM((4, 384, HD), bf16),
            pltpu.VMEM((256, HD), bf16),
            pltpu.VMEM((4, 128), jnp.int32),
            pltpu.VMEM((6, 128, 128), f32),
            pltpu.VMEM((2 * KV, TOK, HD), bf16),
            pltpu.VMEM((2, TOK, KV, HD), bf16),
            pltpu.VMEM((KV, TOK + WINDOW, HD), f32),
            pltpu.VMEM((KV, TOK + WINDOW, HD), f32),
            pltpu.VMEM((KV, 2, WINDOW, HD), bf16),
            pltpu.VMEM((KV, 2, WINDOW, HD), bf16),
            pltpu.VMEM((HALF, 2, 2, WINDOW, HD), bf16),
            pltpu.VMEM((HALF, 2, 2, WINDOW, HD), bf16),
            pltpu.VMEM((TOK, HALF, HD), bf16),
            pltpu.VMEM((TOK, HALF, HD), bf16),
            pltpu.VMEM((2, 384, 256), f32),
            pltpu.VMEM((2, 384, 256), f32),
            pltpu.VMEM((2, 384, 256), f32),
            pltpu.VMEM((2, 384, 256), f32),
            pltpu.VMEM((2, 384, 256), bf16),
            pltpu.VMEM((2, 384, 256), bf16),
            pltpu.VMEM((2, 384, 256), bf16),
            pltpu.VMEM((2, 384, 256), bf16),
            dma((2, 2)),
            dma((2, 2)),
            dma((2, KV)),
            dma((2, KV)),
            dma(()),
            dma(()),
            dma((KV,)),
            dma((KV,)),
            dma((HALF, 2)),
            dma((HALF, 2)),
            dma((2,)),
            dma((2, 2)),
        ],
        compiler_params=pltpu.CompilerParams(
            collective_id=0, has_side_effects=True, vmem_limit_bytes=56 * 1024 * 1024
        ),
        cost_estimate=pl.CostEstimate(flops=8 * 10**9, bytes_accessed=9 * 2**20, transcendentals=3 * 10**6),
    )(
        queries.reshape(TOK, 2, KV, HD), key_heads, value_heads, out_grad.reshape(TOK, 2, KV, HD),
        doc_ids.reshape(4, 128),
    )
    query_grad, key_grad, value_grad = pl.pallas_call(
        deliver,
        out_shape=tuple(jax.ShapeDtypeStruct(p.shape, p.dtype) for p in parts),
        in_specs=[hbm] * 3,
        out_specs=(hbm,) * 3,
        scratch_shapes=[pltpu.VMEM(p.shape, p.dtype) for p in parts] + [dma((3, PIECES)), dma((3, PIECES))],
        compiler_params=pltpu.CompilerParams(vmem_limit_bytes=56 * 1024 * 1024),
    )(*parts)
    return query_grad.reshape(TOK, KV, 2, HD), key_grad, value_grad


def solution(mesh):
    return jax.shard_map(
        on_device,
        mesh=mesh,
        in_specs=(
            P("ctx", None, "head", None),
            P("ctx", None, None),
            P("ctx", None, None),
            P("ctx", None, "head", None),
            P("ctx"),
        ),
        out_specs=(P("ctx", None, "head", None), P("ctx", "head", None), P("ctx", "head", None)),
        check_vma=False,
    )
```

```python
import functools

import jax
import jax.numpy as jnp
from jax import lax
from jax.experimental import pallas as pl
from jax.experimental.pallas import tpu as pltpu
from jax.sharding import PartitionSpec as P

MESH = pl.DeviceIdType.MESH
WINDOW = 256
TOK = 512
KV = 8
HD = 128
HALF = 4
NCTX = 128
TURN = NCTX // 2
SCALE = HD**-0.5
EXP_SCALE = SCALE * 1.4426950408889634
HIDDEN = -1e30
PIECES = 2
CHUNK = 128
NT = (((1,), (1,)), ((), ()))
NN = (((1,), (0,)), ((), ()))
TN = (((0,), (0,)), ((), ()))
bf16 = jnp.bfloat16
f32 = jnp.float32


def dot(a, b, dims):
    return lax.dot_general(a, b, dims, preferred_element_type=f32)


def kernel(
    q_hbm, k_hbm, v_hbm, g_hbm, doc_ref,
    dq_hbm, dk_hbm, dv_hbm,
    q_raw, g_raw, k_raw, v_raw, qt, gt, kt, vt, mask, onehot, doc_halo, doc_col,
    dqt, dq_s, ak, av, edge_s, edge_r, xs, xr, out_k, out_v,
    s_a, s_b, dp_a, dp_b, p_a, p_b, ds_a, ds_b,
    in_sem, kv_sem, f_send, f_recv, d_send, d_recv, e_send, e_recv, x_send, x_recv, dq_sem, out_sem,
):
    c = lax.axis_index("ctx")
    h = lax.axis_index("head")
    par = lax.rem(c, 2)
    first, last = c == 0, c == NCTX - 1
    has_prev, has_next = c > 0, c < NCTX - 1
    before_turn, after_turn = c == TURN - 1, c == TURN
    partner, nxt, prv = (c, 1 - h), (c + 1, h), (c - 1, h)
    nxt_v = (c + 1, jnp.where(before_turn, 1 - h, h))

    def remote(src, dst, send, recv, dev):
        return pltpu.make_async_remote_copy(
            src_ref=src, dst_ref=dst, send_sem=send, recv_sem=recv, device_id=dev, device_id_type=MESH
        )

    def head_of(grp, i):
        return HALF * jnp.where(grp == 0, 1 - h, h) + i

    barrier = pltpu.get_barrier_semaphore()
    pl.semaphore_signal(barrier, inc=1, device_id=partner, device_id_type=MESH)

    @pl.when(has_prev)
    def _():
        pl.semaphore_signal(barrier, inc=1, device_id=prv, device_id_type=MESH)

    @pl.when(par == 0)
    def _():
        pl.semaphore_signal(barrier, inc=1, device_id=nxt, device_id_type=MESH)

    @pl.when(after_turn)
    def _():
        pl.semaphore_signal(barrier, inc=1, device_id=(c - 1, 1 - h), device_id_type=MESH)

    def kv_copy(j, r):
        src, dst = ((k_hbm, k_raw), (v_hbm, v_raw))[j]
        rows = pl.ds(r * WINDOW, WINDOW)
        return pltpu.make_async_copy(src.at[rows], dst.at[rows], kv_sem.at[j, r])

    def qg_copy(j, part):
        src, dst = ((q_hbm, q_raw), (g_hbm, g_raw))[j]
        return pltpu.make_async_copy(src.at[:, part], dst.at[part], in_sem.at[j, part])

    for j in (0, 1):
        kv_copy(j, 1).start()
    for j in (0, 1):
        kv_copy(j, 0).start()
    for part in (1 - h, h):
        for j in (0, 1):
            qg_copy(j, part).start()

    key_row = lax.broadcasted_iota(jnp.int32, (128, 128), 0)
    tok_col = lax.broadcasted_iota(jnp.int32, (128, 128), 1)
    onehot[:128] = jnp.where(key_row == tok_col, 1.0, 0.0).astype(bf16)
    onehot[128:] = jnp.where(key_row == tok_col, 1.0, 0.0).astype(bf16)

    def doc_columns(block, ref, r):
        wide = jnp.broadcast_to(ref[r : r + 1, :], (128, 128)).astype(f32)
        doc_col[block] = wide.T

    def build_mask(t):
        docs = jnp.broadcast_to(doc_ref[t : t + 1, :], (128, 128)).astype(f32)
        for b, inside in enumerate((key_row > tok_col, None, key_row <= tok_col)):
            same = doc_col[t + b] == docs
            seen = same if inside is None else same & inside
            mask[t, b * 128 : (b + 1) * 128] = jnp.where(seen, 0.0, HIDDEN).astype(bf16)

    for b in range(4):
        doc_columns(2 + b, doc_ref, b)
    build_mask(2)
    build_mask(3)

    def clear(n, _):
        ak[n] = jnp.zeros((TOK + WINDOW, HD), f32)
        av[n] = jnp.zeros((TOK + WINDOW, HD), f32)
        return 0

    lax.fori_loop(0, KV, clear, 0)


    @pl.when(first)
    def _():
        kt[:, :WINDOW] = jnp.zeros((KV, WINDOW, HD), bf16)
        vt[:, :WINDOW] = jnp.zeros((KV, WINDOW, HD), bf16)
        doc_halo[...] = jnp.full((4, 128), -1, jnp.int32)

    @pl.when(last)
    def _():
        edge_r[...] = jnp.zeros(edge_r.shape, bf16)

    def swap(src, dst, r):
        def body(b, _):
            t = pl.multiple_of(r * WINDOW + b * CHUNK, CHUNK)
            dst[:, pl.ds(pl.multiple_of(t + WINDOW, CHUNK), CHUNK)] = jnp.swapaxes(src[pl.ds(t, CHUNK)], 0, 1)
            return 0

        lax.fori_loop(0, WINDOW // CHUNK, body, 0)

    for j, src, dst in ((0, k_raw, kt), (1, v_raw, vt)):
        kv_copy(j, 1).wait()
        swap(src, dst, 1)

    def doc_copy():
        return remote(doc_ref, doc_halo, d_send, d_recv, nxt)

    def halo_copy(n, j):
        ref = (kt, vt)[j]
        dev = (nxt, nxt_v)[j]
        return remote(
            ref.at[n, pl.ds(TOK, WINDOW)], ref.at[n, pl.ds(0, WINDOW)], f_send.at[j, n], f_recv.at[j, n], dev
        )

    @pl.when(par == 0)
    def _():
        pl.semaphore_wait(barrier, 2)

    @pl.when((par == 1) & has_next & jnp.logical_not(before_turn))
    def _():
        pl.semaphore_wait(barrier, 3)

    @pl.when(before_turn)
    def _():
        pl.semaphore_wait(barrier, 4)

    @pl.when(last)
    def _():
        pl.semaphore_wait(barrier, 2)

    def send_halo(grp):
        @pl.when(has_next)
        def _():
            def body(i, _):
                n = head_of(grp, i)
                halo_copy(n, 0).start()
                halo_copy(jnp.where(before_turn, lax.rem(n + HALF, KV), n), 1).start()
                return 0

            lax.fori_loop(0, HALF, body, 0)

    @pl.when(has_next)
    def _():
        doc_copy().start()

    send_halo(0)

    for j, src, dst in ((0, k_raw, kt), (1, v_raw, vt)):
        kv_copy(j, 0).wait()
        swap(src, dst, 0)

    def edge_copy(n):
        cross = after_turn & (n // HALF != h)
        slot = jnp.where(cross, lax.rem(n + HALF, KV), n)
        dev = (c - 1, jnp.where(cross, 1 - h, h))
        return remote(edge_s.at[n], edge_r.at[slot], e_send.at[n], e_recv.at[slot], dev)

    def edge_arrival(n):
        return remote(edge_s.at[n], edge_r.at[n], e_send.at[n], e_recv.at[n], prv)

    def x_copy(i, r):
        return remote(xs.at[i, r], xr.at[i, r], x_send.at[i, r], x_recv.at[i, r], partner)

    def dq_copy(part):
        return pltpu.make_async_copy(dq_s.at[part], dq_hbm.at[:, part], dq_sem.at[part])

    def swap_in(part):
        for j, src, dst in ((0, q_raw, qt), (1, g_raw, gt)):
            qg_copy(j, part).wait()

            def body(b, _, src=src, dst=dst):
                t = pl.ds(pl.multiple_of(b * CHUNK, CHUNK), CHUNK)
                dst[pl.ds(part * KV, KV), t] = jnp.swapaxes(src[part, t], 0, 1)
                return 0

            lax.fori_loop(0, TOK // CHUNK, body, 0)

    def swap_out(part):
        def body(b, _):
            t = pl.ds(pl.multiple_of(b * CHUNK, CHUNK), CHUNK)
            dq_s[part, t] = jnp.swapaxes(dqt[pl.ds(part * KV, KV), t], 0, 1)
            return 0

        lax.fori_loop(0, TOK // CHUNK, body, 0)
        dq_copy(part).start()

    def send_tail_sums(i):
        n = head_of(0, i)

        @pl.when(before_turn)
        def _():
            xs[i, 1, 0] = (ak[n, TOK:] * SCALE).astype(bf16)
            xs[i, 1, 1] = av[n, TOK:].astype(bf16)

        @pl.when(jnp.logical_not(before_turn))
        def _():
            @pl.when(has_next)
            def _():
                edge_arrival(n).wait_recv()

            xs[i, 1, 0] = (ak[n, TOK:] * SCALE + edge_r[n, 0].astype(f32)).astype(bf16)
            xs[i, 1, 1] = (av[n, TOK:] + edge_r[n, 1].astype(f32)).astype(bf16)

        x_copy(i, 1).start()

    def plan(s):
        i = lax.rem(s, HALF)
        grp = s // (2 * HALF)
        late = lax.rem(s // HALF + jnp.where((grp == 1) & (par == 0), 1, 0), 2)
        t0 = 2 * jnp.where(late == 1, par, 1 - par)
        return i, late, grp, head_of(grp, i), t0, late + par == 1

    def places(n, t0, j):
        t = t0 + j
        toks = pl.ds(pl.multiple_of(t * 128, 128), 128)
        keys = pl.ds(pl.multiple_of(t * 128, 128), 384)
        return t, (pl.ds(2 * n, 2), toks), keys

    def prepare(s):
        i, _, grp, n, _, crossing = plan(s)

        @pl.when(s == 2 * HALF)
        def _():
            swap_in(h)

        @pl.when(crossing & (i == 0) & (grp == 0))
        def _():
            @pl.when(has_prev)
            def _():
                doc_copy().wait_recv()

            doc_columns(0, doc_halo, 2)
            doc_columns(1, doc_halo, 3)
            build_mask(0)
            build_mask(1)

        @pl.when(crossing & has_prev)
        def _():
            halo_copy(n, 0).wait_recv()
            halo_copy(n, 1).wait_recv()

    def front(s, s_to, dp_to):
        _, _, _, n, t0, _ = plan(s)
        for j in range(2):
            t, where, keys = places(n, t0, j)
            q = qt[where].reshape(256, HD)
            s_to[j] = dot(jnp.concatenate([kt[n, keys], mask[t]], 1), jnp.concatenate([q, onehot[...]], 1), NT)
            yield
            dp_to[j] = dot(vt[n, keys], gt[where].reshape(256, HD), NT)
            yield

    def middle(s_of, dp_of, p_to, ds_to):
        for j in range(2):
            for part in (slice(0, 128), slice(128, 256)):
                scores = s_of[j, :, part]
                dp = dp_of[j, :, part]
                top = jnp.max(scores, 0, keepdims=True)
                e = jnp.exp2((scores - top) * EXP_SCALE)
                total = jnp.sum(e, 0, keepdims=True)
                moment = jnp.sum(e * dp, 0, keepdims=True)
                inv = 1.0 / total
                p = e * inv
                ds_to[j, :, part] = (p * (dp - moment * inv)).astype(bf16)
                p_to[j, :, part] = p.astype(bf16)
                yield

    def back(s, p_of, ds_of):
        _, _, _, n, t0, _ = plan(s)
        for j in range(2):
            _, where, keys = places(n, t0, j)
            ds = ds_of[j]
            ak[n, keys] += dot(ds, qt[where].reshape(256, HD), NN)
            av[n, keys] += dot(p_of[j], gt[where].reshape(256, HD), NN)
            yield
            dq = (dot(kt[n, keys], ds, TN) * SCALE).T.astype(bf16)
            dqt[where] = dq.reshape(2, 128, HD)
            yield

    def weave(*works):
        works = list(works)
        while works:
            works = [w for w in works if next(w, True) is None]

    def pass_on(s):
        i, late, grp, n, _, crossing = plan(s)

        @pl.when(crossing & has_prev)
        def _():
            edge_s[n, 0] = (ak[n, :WINDOW] * SCALE).astype(bf16)
            edge_s[n, 1] = av[n, :WINDOW].astype(bf16)
            edge_copy(n).start()

        @pl.when((late == 1) & (grp == 0))
        def _():
            xs[i, 0, 0] = (ak[n, WINDOW:TOK] * SCALE).astype(bf16)
            xs[i, 0, 1] = av[n, WINDOW:TOK].astype(bf16)
            x_copy(i, 0).start()

        @pl.when((par == 0) & (s < HALF))
        def _():
            send_tail_sums(s)

        @pl.when((par == 1) & (s >= 2 * HALF) & (s < 3 * HALF))
        def _():
            send_tail_sums(s - 2 * HALF)

        @pl.when(s == 2 * HALF - 1)
        def _():
            swap_out(1 - h)

    steps = 4 * HALF
    slots = ((s_a, dp_a, p_a, ds_a), (s_b, dp_b, p_b, ds_b))
    swap_in(1 - h)
    prepare(0)
    weave(front(0, s_a, dp_a))
    send_halo(1)

    prepare(1)
    weave(middle(*slots[0]), front(1, s_b, dp_b))

    def pair(at, _):
        for k in range(2):
            s = 2 * at + k + 1
            here, other = slots[1 - k], slots[k]
            prepare(s + 1)
            weave(middle(*here), back(s - 1, other[2], other[3]), front(s + 1, other[0], other[1]))
            pass_on(s - 1)
        return 0

    lax.fori_loop(0, steps // 2 - 1, pair, 0)
    weave(middle(*slots[1]), back(steps - 2, p_a, ds_a))
    pass_on(steps - 2)
    weave(back(steps - 1, p_b, ds_b))
    pass_on(steps - 1)
    swap_out(h)

    def out_copy(j, r):
        src, dst = ((out_k, dk_hbm), (out_v, dv_hbm))[j]
        rows = pl.ds(r * WINDOW, WINDOW)
        return pltpu.make_async_copy(src.at[rows], dst.at[rows], out_sem.at[j, r])

    def finish(r):
        def wait_head(i, _):
            x_copy(i, r).wait_recv()
            if r == 1:

                @pl.when(has_next)
                def _():
                    edge_arrival(HALF * h + i).wait_recv()

                @pl.when(before_turn)
                def _():
                    n, slot = head_of(1, i), head_of(0, i)
                    edge_arrival(slot).wait_recv()
                    ak[n, TOK:] += edge_r[slot, 0].astype(f32) * (1.0 / SCALE)
                    av[n, TOK:] += edge_r[slot, 1].astype(f32)

            return 0

        lax.fori_loop(0, HALF, wait_head, 0)
        own = pl.ds(HALF * h, HALF)

        def body(b, _):
            t = pl.multiple_of(b * CHUNK, CHUNK)
            part = pl.ds(t, CHUNK)
            accs = pl.ds(pl.multiple_of((r + 1) * WINDOW + t, CHUNK), CHUNK)
            outs = pl.ds(pl.multiple_of(r * WINDOW + t, CHUNK), CHUNK)
            for j, acc, scale, out in ((0, ak, SCALE, out_k), (1, av, None, out_v)):
                val = acc[own, accs]
                if scale is not None:
                    val = val * scale
                val = val + xr[:, r, j, part].astype(f32)
                if r == 1:
                    val = val + edge_r[own, j, part].astype(f32)
                out[outs] = jnp.swapaxes(val.astype(bf16), 0, 1)
            return 0

        lax.fori_loop(0, WINDOW // CHUNK, body, 0)
        out_copy(0, r).start()
        out_copy(1, r).start()

    @pl.when(par == 0)
    def _():
        finish(1)
        finish(0)

    @pl.when(par == 1)
    def _():
        finish(0)
        finish(1)

    @pl.when(has_next)
    def _():
        doc_copy().wait_send()

    def drain(n, _):
        @pl.when(has_next)
        def _():
            halo_copy(n, 0).wait_send()
            halo_copy(n, 1).wait_send()

        @pl.when(has_prev)
        def _():
            edge_copy(n).wait_send()

        return 0

    lax.fori_loop(0, KV, drain, 0)
    for part in range(2):
        dq_copy(part).wait()

    def drain_x(i, _):
        for r in range(2):
            x_copy(i, r).wait_send()
        return 0

    lax.fori_loop(0, HALF, drain_x, 0)
    for r in range(2):
        for j in range(2):
            out_copy(j, r).wait()


def deliver(dq_in, dk_in, dv_in, dq_out, dk_out, dv_out, dq_v, dk_v, dv_v, in_sem, out_sem):
    ways = ((dq_in, dq_v, dq_out), (dk_in, dk_v, dk_out), (dv_in, dv_v, dv_out))
    moves = []
    for j in range(PIECES):
        rows = pl.ds(j * (TOK // PIECES), TOK // PIECES)
        for a, (src, mid, dst) in enumerate(ways):
            moves.append((
                pltpu.make_async_copy(src.at[rows], mid.at[rows], in_sem.at[a, j]),
                pltpu.make_async_copy(mid.at[rows], dst.at[rows], out_sem.at[a, j]),
            ))
    for load, _ in moves:
        load.start()
    for load, store in moves:
        load.wait()
        store.start()
    for _, store in moves:
        store.wait()


def on_device(queries, key_heads, value_heads, out_grad, doc_ids):
    hbm = pl.BlockSpec(memory_space=pl.ANY)
    vmem = pl.BlockSpec(memory_space=pltpu.VMEM)
    dma = pltpu.SemaphoreType.DMA
    parts = pl.pallas_call(
        kernel,
        out_shape=(
            jax.ShapeDtypeStruct((TOK, 2, KV, HD), bf16),
            jax.ShapeDtypeStruct((TOK, HALF, HD), bf16),
            jax.ShapeDtypeStruct((TOK, HALF, HD), bf16),
        ),
        in_specs=[hbm, hbm, hbm, hbm, vmem],
        out_specs=(hbm, hbm, hbm),
        scratch_shapes=[
            pltpu.VMEM((2, TOK, KV, HD), bf16),
            pltpu.VMEM((2, TOK, KV, HD), bf16),
            pltpu.VMEM((TOK, KV, HD), bf16),
            pltpu.VMEM((TOK, KV, HD), bf16),
            pltpu.VMEM((2 * KV, TOK, HD), bf16),
            pltpu.VMEM((2 * KV, TOK, HD), bf16),
            pltpu.VMEM((KV, TOK + WINDOW, HD), bf16),
            pltpu.VMEM((KV, TOK + WINDOW, HD), bf16),
            pltpu.VMEM((4, 384, HD), bf16),
            pltpu.VMEM((256, HD), bf16),
            pltpu.VMEM((4, 128), jnp.int32),
            pltpu.VMEM((6, 128, 128), f32),
            pltpu.VMEM((2 * KV, TOK, HD), bf16),
            pltpu.VMEM((2, TOK, KV, HD), bf16),
            pltpu.VMEM((KV, TOK + WINDOW, HD), f32),
            pltpu.VMEM((KV, TOK + WINDOW, HD), f32),
            pltpu.VMEM((KV, 2, WINDOW, HD), bf16),
            pltpu.VMEM((KV, 2, WINDOW, HD), bf16),
            pltpu.VMEM((HALF, 2, 2, WINDOW, HD), bf16),
            pltpu.VMEM((HALF, 2, 2, WINDOW, HD), bf16),
            pltpu.VMEM((TOK, HALF, HD), bf16),
            pltpu.VMEM((TOK, HALF, HD), bf16),
            pltpu.VMEM((2, 384, 256), f32),
            pltpu.VMEM((2, 384, 256), f32),
            pltpu.VMEM((2, 384, 256), f32),
            pltpu.VMEM((2, 384, 256), f32),
            pltpu.VMEM((2, 384, 256), bf16),
            pltpu.VMEM((2, 384, 256), bf16),
            pltpu.VMEM((2, 384, 256), bf16),
            pltpu.VMEM((2, 384, 256), bf16),
            dma((2, 2)),
            dma((2, 2)),
            dma((2, KV)),
            dma((2, KV)),
            dma(()),
            dma(()),
            dma((KV,)),
            dma((KV,)),
            dma((HALF, 2)),
            dma((HALF, 2)),
            dma((2,)),
            dma((2, 2)),
        ],
        compiler_params=pltpu.CompilerParams(
            collective_id=0, has_side_effects=True, vmem_limit_bytes=56 * 1024 * 1024
        ),
        cost_estimate=pl.CostEstimate(flops=8 * 10**9, bytes_accessed=9 * 2**20, transcendentals=3 * 10**6),
    )(
        queries.reshape(TOK, 2, KV, HD), key_heads, value_heads, out_grad.reshape(TOK, 2, KV, HD),
        doc_ids.reshape(4, 128),
    )
    query_grad, key_grad, value_grad = pl.pallas_call(
        deliver,
        out_shape=tuple(jax.ShapeDtypeStruct(p.shape, p.dtype) for p in parts),
        in_specs=[hbm] * 3,
        out_specs=(hbm,) * 3,
        scratch_shapes=[pltpu.VMEM(p.shape, p.dtype) for p in parts] + [dma((3, PIECES)), dma((3, PIECES))],
        compiler_params=pltpu.CompilerParams(vmem_limit_bytes=56 * 1024 * 1024),
    )(*parts)
    return query_grad.reshape(TOK, KV, 2, HD), key_grad, value_grad


def solution(mesh):
    return jax.shard_map(
        on_device,
        mesh=mesh,
        in_specs=(
            P("ctx", None, "head", None),
            P("ctx", None, None),
            P("ctx", None, None),
            P("ctx", None, "head", None),
            P("ctx"),
        ),
        out_specs=(P("ctx", None, "head", None), P("ctx", "head", None), P("ctx", "head", None)),
        check_vma=False,
    )
```
